256 devices in a mesh: grp: 32 (over z, y_hi, core), patch: 8 (over y_lo, x).
Axes of the slice: x: 4, y: 4 (y_hi: 2, y_lo: 2; y = y_hi * 2 + y_lo), z: 8, core: 2. Of those that a mesh axis runs over, the one named last changes fastest.
Arguments:
- latent: bfloat16 [32768, 1536], P(('grp', 'patch')), may hold values from -24 to 24
- incoming: int32 [8, 32], P('patch', 'grp'), may hold values from 0 to 31, each once within a row
- req_pages: int32 [32, 4], P('grp'), may hold values from 1 to 48, 64 in all within a row
- text_len: int32 [32, 4], P('grp'), may hold values from 1 to 128, as said below
- gate_scale: float32 [32, 4, 1536], P('grp'), may hold values from 0.2 to 1.2
- text_keys: bfloat16 [32, 4, 128, 1536], P('grp'), may hold values from -6 to 6
- text_values: bfloat16 [32, 4, 128, 1536], P('grp'), may hold values from -6 to 6
- w_query: bfloat16 [1536, 1536], P('grp'), may hold values from -0.25 to 0.25
- w_key: bfloat16 [1536, 1536], P('grp'), may hold values from -0.25 to 0.25
- w_value: bfloat16 [1536, 1536], P('grp'), may hold values from -0.15625 to 0.15625
- w_out: bfloat16 [1536, 1536], replicated, may hold values from -0.15625 to 0.15625
Outputs:
- denoised: bfloat16 [32768, 1536], P(('grp', 'patch'))
The draws below stay inside these ranges and needn't reach their ends.
Inputs may be any that keep to these rules, and one draw needn't show every extreme that they name: `incoming`: each row is a permutation. `req_pages`: A group's counts sum to 64, and in every group one request holds exactly 48 pages. `text_len`: in every group one request has all 128 text tokens live.
All inputs are finite; a program needn't handle non-finite values.
Results may differ from the reference program's by a relative error of at most 0.03.
The reference program's roundings to bfloat16 on the way count: a program that leaves them out, or rounds other values in their place, can miss the bound.
Values may be sent and summed in bfloat16 or wider, within the bound.
A program may use at most 128 MiB of HBM per device.

```python
import math
import jax
import jax.numpy as jnp
import numpy as np
from jax import lax

HEADS = 12
HEAD_DIM = 128
WIDTH = 1536
TOK_DEV = 128
PAGE = 16
OUT = 1
REQS = 4
TXT = 128
STEPS = 2
TOKENS = 32768
GPAGES = 64
BIG = 48
N_GRP = 32
N_PATCH = 8


def draw_latent(key, part):
    key = jax.random.fold_in(key, 11)
    array_shape = (TOKENS, HEADS * HEAD_DIM)
    values = jnp.clip(jax.random.normal(key, array_shape, jnp.float32), -4.0, 4.0)
    return values.astype(jnp.bfloat16)


def draw_text_len(key, part):
    key = jax.random.fold_in(key, 23)
    length_key, pick_key = jax.random.split(key)
    lengths_drawn = jax.random.randint(length_key, (N_GRP, REQS), 1, TXT + 1, dtype=jnp.int32)
    chosen_req = jax.random.randint(pick_key, (N_GRP, 1), 0, REQS, dtype=jnp.int32)
    columns = jnp.arange(REQS, dtype=jnp.int32)[None, :]
    return jnp.where(columns == chosen_req, TXT, lengths_drawn).astype(jnp.int32)


def block_scale(stream_key, shape, cuts, least, largest):
    factor_of, own = 1.0, jax.random.fold_in(stream_key, 6)
    for axis_at, parts in cuts:
        draws = jnp.exp(jax.random.uniform(jax.random.fold_in(own, axis_at), (parts,), jnp.float32, least / len(cuts), largest / len(cuts)))
        factor_of = factor_of * jnp.repeat(draws, shape[axis_at] // parts).reshape([-1 if axis == axis_at else 1 for axis in range(len(shape))])
    return factor_of


def profile(count, total, reach, skew):
    portions = [(1 << 20) // math.isqrt(rank ** skew) + 1 for rank in range(2, count + 1)]
    surplus, given = total - reach - (count - 1), [1] * (count - 1)
    while surplus > 0:
        candidates = [i for i in range(count - 1) if given[i] < reach]
        pool, remaining = sum([portions[i] for i in candidates]), surplus
        for i in candidates:
            extra = min(reach - given[i], max(1, remaining * portions[i] // pool), surplus)
            given[i] = given[i] + extra
            surplus = surplus - extra
    return np.array([reach] + given)


def ragged(own_key, count, total, bound, lean):
    if count == 2:
        one = jax.random.randint(own_key, (), max(1, total - bound), min(bound, total - 1) + 1)
        return jnp.stack([one, total - one])
    sizes = jnp.asarray(profile(count, total, bound, lean), jnp.int32)
    couples = (count - 1) // 2
    source_of, receiver = sizes[1:1 + 2 * couples:2], sizes[2:2 + 2 * couples:2]
    slack = jnp.minimum(source_of - 1, bound - receiver)
    passed = jax.random.randint(jax.random.fold_in(own_key, 1), (couples,), 0, 1 << 20) % (slack + 1)
    sizes = sizes.at[1:1 + 2 * couples:2].set(source_of - passed).at[2:2 + 2 * couples:2].set(receiver + passed)
    return sizes[jax.random.permutation(jax.random.fold_in(own_key, 2), count)]


def scatter_about(key, shape, width, reach, cuts=(), held_as=jnp.bfloat16):
    loudness = block_scale(key, shape, cuts, -0.22, 0.18) if cuts else 1.0
    values = jax.random.normal(key, shape, jnp.float32) * width * loudness
    return jnp.minimum(jnp.maximum(values, -reach), reach).astype(held_as)


def setup_inputs(seed: int = 0) -> dict:
    seeds = jax.random.split(jax.random.key(seed), 12)
    latent = draw_latent(jax.random.fold_in(seeds[11], 71), 0)
    incoming = jax.vmap(lambda own: jax.random.permutation(own, N_GRP * OUT))(jax.random.split(seeds[1], N_PATCH)).reshape((N_PATCH, N_GRP * OUT)).astype(jnp.int32)
    req_pages = jax.vmap(lambda own: ragged(own, REQS, GPAGES, BIG, 2))(jax.random.split(seeds[2], N_GRP)).reshape((N_GRP, REQS)).astype(jnp.int32)
    text_len = draw_text_len(jax.random.fold_in(seeds[11], 71), 0)
    gate_scale = jnp.clip(0.2 + 1 * jax.random.uniform(seeds[4], (N_GRP, REQS, WIDTH), jnp.float32) ** block_scale(seeds[4], (N_GRP, REQS, WIDTH), ((0, 32),), -0.2, 0.2), 0.2, 1.2)
    text_keys = scatter_about(seeds[5], (N_GRP, REQS, TXT, WIDTH), 1.0, 6.0, ((0, 32),))
    text_values = scatter_about(seeds[6], (N_GRP, REQS, TXT, WIDTH), 1.0, 6.0, ((0, 32),))
    w_query = scatter_about(seeds[7], (WIDTH, WIDTH), (WIDTH // 3) ** -0.5, 0.25, ((0, 32),))
    w_key = scatter_about(seeds[8], (WIDTH, WIDTH), (WIDTH // 3) ** -0.5, 0.25, ((0, 32),))
    w_value = scatter_about(seeds[9], (WIDTH, WIDTH), WIDTH ** -0.5, 0.15625, ((0, 32),))
    w_out = scatter_about(seeds[10], (WIDTH, WIDTH), WIDTH ** -0.5, 0.15625)
    return {"latent": latent, "incoming": incoming, "req_pages": req_pages, "text_len": text_len, "gate_scale": gate_scale, "text_keys": text_keys, "text_values": text_values, "w_query": w_query, "w_key": w_key, "w_value": w_value, "w_out": w_out}


NEG_FILL = -1e30


def rounded(values):
    return lax.optimization_barrier(values.astype(jnp.bfloat16)).astype(jnp.float32)


def segment_of(positions, req_row):
    page_ends = (jnp.cumsum(req_row) * PAGE).astype(jnp.int32)
    hits = (positions[:, None] >= page_ends[None, :]).astype(jnp.int32)
    return jnp.sum(hits, axis=1).astype(jnp.int32)


def heads_of(flat_rows):
    return flat_rows.reshape(flat_rows.shape[0], HEADS, HEAD_DIM).transpose(1, 0, 2)


def block_update(hidden, segment, text_row, gate_rows, keys_text, values_text, w_query, w_key, w_value, w_out):
    token_count = hidden.shape[0]
    query_heads = heads_of(rounded(jnp.dot(hidden, w_query, preferred_element_type=jnp.float32)))
    key_heads = heads_of(rounded(jnp.dot(hidden, w_key, preferred_element_type=jnp.float32)))
    value_heads = heads_of(rounded(jnp.dot(hidden, w_value, preferred_element_type=jnp.float32)))
    score_scale = 1.0 / (HEAD_DIM ** 0.5)
    image_scores = jnp.einsum("htd,hsd->hts", query_heads, key_heads) * score_scale
    same_request = segment[:, None] == segment[None, :]
    image_scores = jnp.where(same_request[None], image_scores, NEG_FILL)
    text_k = keys_text.astype(jnp.float32).reshape(REQS, TXT, HEADS, HEAD_DIM)
    text_v = values_text.astype(jnp.float32).reshape(REQS * TXT, HEADS, HEAD_DIM).transpose(1, 0, 2)
    text_scores = jnp.einsum("htd,rjhd->htrj", query_heads, text_k) * score_scale
    owner_mask = segment[:, None] == jnp.arange(REQS, dtype=jnp.int32)[None, :]
    live_text = jnp.arange(TXT, dtype=jnp.int32)[None, :] < text_row[:, None]
    allowed = owner_mask[:, :, None] & live_text[None]
    text_scores = jnp.where(allowed[None], text_scores, NEG_FILL).reshape(HEADS, token_count, REQS * TXT)
    scores = jnp.concatenate([text_scores, image_scores], axis=2)
    row_max = jnp.max(scores, axis=2, keepdims=True)
    weights = jnp.exp(scores - row_max)
    totals = jnp.sum(weights, axis=2)
    all_values = jnp.concatenate([text_v, value_heads], axis=1)
    mixed_heads = jnp.einsum("hts,hsd->htd", rounded(weights), all_values) / totals[:, :, None]
    mixed_flat = mixed_heads.transpose(1, 0, 2).reshape(token_count, HEADS * HEAD_DIM).astype(jnp.bfloat16)
    projected = jnp.dot(mixed_flat, w_out, preferred_element_type=jnp.float32)
    return (hidden.astype(jnp.float32) + gate_rows[segment] * projected).astype(jnp.bfloat16)


def take_rows(pool_rows, order_rows):
    return pool_rows[order_rows]


def reference(latent, incoming, req_pages, text_len, gate_scale, text_keys, text_values, w_query, w_key, w_value, w_out):
    pages_dev = TOK_DEV // PAGE
    keep_pages = pages_dev - OUT
    channels = HEADS * HEAD_DIM
    arrival = latent.reshape(N_GRP, N_PATCH, pages_dev, PAGE, channels)
    leaving_pool = arrival[:, :, keep_pages:].transpose(1, 0, 2, 3, 4).reshape(N_PATCH, N_GRP * OUT, PAGE, channels)
    picked = jax.vmap(take_rows)(leaving_pool, incoming)
    picked = picked.reshape(N_PATCH, N_GRP, OUT, PAGE, channels).transpose(1, 0, 2, 3, 4)
    state = jnp.concatenate([arrival[:, :, :keep_pages], picked], axis=2).reshape(N_GRP, N_PATCH * TOK_DEV, channels)
    positions = jnp.arange(N_PATCH * TOK_DEV, dtype=jnp.int32)

    def one_group(group_args):
        hidden, req_row, text_row, gate_rows, keys_text, values_text = group_args
        segment = segment_of(positions, req_row)
        for step_index in range(STEPS):
            hidden = block_update(hidden, segment, text_row, gate_rows, keys_text, values_text, w_query, w_key, w_value, w_out)
        return hidden

    state = lax.map(one_group, (state, req_pages, text_len, gate_scale, text_keys, text_values))
    placed = state.reshape(N_GRP, N_PATCH, pages_dev, PAGE, channels)
    pool_back = placed[:, :, keep_pages:].transpose(1, 0, 2, 3, 4).reshape(N_PATCH, N_GRP * OUT, PAGE, channels)
    inverse = jnp.argsort(incoming, axis=1).astype(jnp.int32)
    returned = jax.vmap(take_rows)(pool_back, inverse)
    returned = returned.reshape(N_PATCH, N_GRP, OUT, PAGE, channels).transpose(1, 0, 2, 3, 4)
    result = jnp.concatenate([placed[:, :, :keep_pages], returned], axis=2)
    return result.reshape(N_GRP * N_PATCH * TOK_DEV, channels)
```

```python
import math

import jax
import jax.numpy as jnp
from jax import lax
from jax.experimental import pallas as pl
from jax.experimental.pallas import tpu as pltpu
from jax.sharding import PartitionSpec as P

MESH = pl.DeviceIdType.MESH
HEADS = 12
DIM = 128
WIDTH = 1536
PAGE = 16
REQS = 4
TXT = 128
TOK = 128
SEQ = 1024
KEEP = TOK - PAGE
NZ = 8
WROWS = 48
KEYS = SEQ + REQS * TXT
QB = 256
NEG_FILL = -1e30
TAG = 128
F32 = jnp.float32
BF16 = jnp.bfloat16
EXP_SCALE = math.log2(math.e) / math.sqrt(DIM)

PARTS = ((0, 64), (64, 48), (112, 16))


def kernel(
    lat, inc, req_pages, text_len, gate, text_k, text_v, w_q, w_k, w_v, w_o, out,
    hid, wgt, wout, mix, keys, vals, qry, mine, fin, kid,
    pages, back, ints, pick_out, pick_in,
    local_sem, z_send, z_recv, swap_send, swap_recv, yh_send, yh_recv,
    set_send, set_recv, hg_send, hg_recv, mg_send, mg_recv, aa_send, aa_recv,
):
    g = lax.axis_index("grp")
    p = lax.axis_index("patch")
    z, c = g // 4, g % 4
    x, yl = p % 4, p // 4

    def patch_of(dx, dy):
        return ((yl + dy) % 2) * 4 + (x + dx) % 4

    right, left, other = (g, patch_of(1, 0)), (g, patch_of(3, 0)), (g, patch_of(0, 1))
    up, down = ((g + 4) % 32, p), ((g + 28) % 32, p)
    core_g = (g // 2) * 2 + 1 - g % 2
    yhi_g = z * 4 + (c + 2) % 4
    core, yhi = (core_g, p), (yhi_g, p)

    def set_peer(j):
        return z * 4 + (c + j) % 4

    def zdev(dz, cc):
        return ((z + dz) % NZ) * 4 + cc

    head_a = p
    head_b = 8 + p // 2
    col_a = pl.ds(pl.multiple_of(head_a * DIM, DIM), DIM)
    col_b = pl.ds(pl.multiple_of(head_b * DIM, DIM), DIM)

    def wrows(gg):
        return wgt.at[pl.ds(pl.multiple_of(gg * WROWS, 16), WROWS), :]

    loads = []
    my_rows = pl.ds(pl.multiple_of(g * WROWS, 16), WROWS)
    for n, w in enumerate((w_q, w_k, w_v)):
        for m, col in enumerate((col_a, col_b)):
            loads.append(pltpu.make_async_copy(
                w.at[:, col], wgt.at[my_rows, pl.ds((2 * n + m) * DIM, DIM)], local_sem.at[2 * n + m]))
    text_loads = []
    for n, (src, dst) in enumerate(((text_k, keys), (text_v, vals))):
        for m, col in enumerate((col_a, col_b)):
            text_loads.append(pltpu.make_async_copy(
                src.at[:, col], dst.at[m, pl.ds(SEQ, REQS * TXT), :], local_sem.at[6 + 2 * n + m]))
    my_hid = pl.ds(pl.multiple_of(p * TOK, TOK), KEEP)
    text_loads.append(pltpu.make_async_copy(lat.at[pl.ds(0, KEEP), :], hid.at[my_hid, :], local_sem.at[10]))
    wout_load = pltpu.make_async_copy(w_o, wout, local_sem.at[11])
    page_load = pltpu.make_async_copy(lat.at[pl.ds(KEEP, PAGE), :], pages.at[z], local_sem.at[12])
    for load in loads:
        load.start()
    page_load.start()
    ints[g] = jnp.full((8, 128), inc[0, 0], jnp.int32)

    barrier = pltpu.get_barrier_semaphore()
    greeted = [up, down] + [(set_peer(j), p) for j in (1, 2, 3)]
    greeted += [(g, patch_of(dx, dy)) for dy in (0, 1) for dx in range(4) if (dx, dy) != (0, 0)]
    for peer in greeted:
        pl.semaphore_signal(barrier, inc=1, device_id=peer, device_id_type=MESH)
    pl.semaphore_wait(barrier, len(greeted))

    pending = []

    def remote(src, dst, send, recv, dev):
        return pltpu.make_async_remote_copy(
            src_ref=src, dst_ref=dst, send_sem=send, recv_sem=recv, device_id=dev, device_id_type=MESH)

    def go(*args):
        copy = remote(*args)
        copy.start()
        pending.append(copy)

    Z_FROM = (-1, -2, -3, 1, 2, 3, 4)

    def z_copy(item, at, slot, dz, dev):
        return remote(at(dz), at(dz), z_send.at[item, slot], z_recv.at[item, slot], dev)

    def z_go(item, at, slot, dz, dev):
        copy = z_copy(item, at, slot, dz, dev)
        copy.start()
        pending.append(copy)

    def z_wait(item, at, slot):
        z_copy(item, at, slot, Z_FROM[slot], up).wait_recv()

    def z_first(item, at):
        z_go(item, at, 0, 0, up)
        z_go(item, at, 3, 0, down)

    def z_step(item, at, step, last_up):
        if step == 4:
            z_wait(item, at, 6)
            return
        z_wait(item, at, step - 1)
        if step < 3:
            z_go(item, at, step, -step, up)
        elif last_up:
            z_go(item, at, 6, -3, up)
        z_wait(item, at, 2 + step)
        if step < 3:
            z_go(item, at, 3 + step, step, down)
        elif not last_up:
            z_go(item, at, 6, 3, down)

    def page_at(dz):
        return pages.at[(z + dz) % NZ]

    def back_at(dz):
        return back.at[(z + dz) % NZ]

    def own_w(dz):
        return wrows(zdev(dz, c))

    def yhi_w(dz):
        return wrows(zdev(dz, (c + 2) % 4))

    def swap(item, dz):
        cc = (c + 2 * item) % 4
        ref = wrows(zdev(dz, cc))
        go(ref, ref, swap_send.at[item, dz % NZ], swap_recv.at[item, dz % NZ], core)

    def swap_wait(item, dz):
        other_c = (c // 2) * 2 + 1 - c % 2
        ref = wrows(zdev(dz, (other_c + 2 * item) % 4))
        remote(ref, ref, swap_send.at[item, dz % NZ], swap_recv.at[item, dz % NZ], core).wait_recv()

    G_FROM = ((3, 0), (1, 0), (0, 1), (2, 0), (3, 1), (1, 1), (2, 1))

    class Gather:
        def __init__(self, send, recv, at):
            self.send, self.recv, self.at = send, recv, at

        def copy(self, k, slot, ps, dev, src=None):
            ref = self.at(k, ps)
            return remote(ref if src is None else src, ref, self.send.at[k, slot], self.recv.at[k, slot], dev)

        def go(self, k, slot, ps, dev, src=None):
            copy = self.copy(k, slot, ps, dev, src)
            copy.start()

        def first(self, k, src=None):
            self.go(k, 0, p, right, src)
            self.go(k, 1, p, left, src)
            self.go(k, 2, p, other, src)

        def wait(self, k, slot):
            self.copy(k, slot, patch_of(*G_FROM[slot]), other).wait_recv()

        def second(self, k, far_right):
            self.wait(k, 0)
            if far_right is True:
                self.go(k, 3, patch_of(3, 0), right)
            self.wait(k, 1)
            if far_right is False:
                self.go(k, 3, patch_of(1, 0), left)
            if far_right is not True and far_right is not False:
                @pl.when(far_right)
                def _():
                    self.go(k, 3, patch_of(3, 0), right)

                @pl.when(jnp.logical_not(far_right))
                def _():
                    self.go(k, 3, patch_of(1, 0), left)
            self.wait(k, 2)
            self.go(k, 4, patch_of(0, 1), right)
            self.go(k, 5, patch_of(0, 1), left)

        def third(self, k):
            self.wait(k, 3)
            self.go(k, 6, patch_of(2, 0), other)

        def last(self, k):
            self.wait(k, 4)
            self.wait(k, 5)
            self.wait(k, 6)

        def drain(self, k):
            for slot in range(7):
                self.copy(k, slot, p, other).wait_send()

    def hid_at(k, ps):
        first, rows = PARTS[k]
        return hid.at[pl.ds(pl.multiple_of(ps * TOK + first, 16), rows), :]

    hg = Gather(hg_send, hg_recv, hid_at)

    page_load.wait()
    z_first(0, page_at)
    for j in (1, 2, 3):
        go(ints.at[g], ints.at[g], set_send.at[0, j - 1], set_recv.at[0, j - 1], (set_peer(j), p))
    hg.first(0, lat.at[pl.ds(0, 64), :])
    hg.first(1, lat.at[pl.ds(64, 48), :])
    for load in loads:
        load.wait()
    go(wrows(g), wrows(g), yh_send, yh_recv, yhi)
    z_first(1, own_w)
    swap(0, 0)
    for load in text_loads:
        load.start()
    wout_load.start()

    ends = []
    total = jnp.int32(0)
    for r in range(REQS):
        total = total + req_pages[0, r] * PAGE
        ends.append(total)

    def segment(pos):
        seg = jnp.zeros(pos.shape, jnp.int32)
        for r in range(REQS):
            seg = seg + (pos >= ends[r]).astype(jnp.int32)
        return seg

    kid[:, 0:SEQ] = segment(lax.broadcasted_iota(jnp.int32, (8, SEQ), 1))
    for r in range(REQS):
        j = lax.broadcasted_iota(jnp.int32, (8, TXT), 1)
        kid[:, SEQ + r * TXT:SEQ + (r + 1) * TXT] = jnp.where(j < text_len[0, r], r, -1)

    z_step(0, page_at, 1, True)
    remote(wrows(yhi_g), wrows(yhi_g), yh_send, yh_recv, yhi).wait_recv()
    z_first(2, yhi_w)
    swap(1, 0)
    z_step(0, page_at, 2, True)
    z_step(0, page_at, 3, True)
    z_step(1, own_w, 1, True)
    z_step(0, page_at, 4, True)

    def route(ring, kind, want):
        own = None
        for j in (1, 2, 3, 0):
            acc = jnp.zeros((PAGE, WIDTH), F32)
            for zz in range(NZ):
                page = ring[zz, :, 0:WIDTH].astype(F32)
                acc = acc + jnp.where(want(zz, j), page, 0.0)
            if j:
                pick_out[kind, j - 1] = acc.astype(BF16)
                go(pick_out.at[kind, j - 1], pick_in.at[kind, j - 1],
                   set_send.at[1 + kind, j - 1], set_recv.at[1 + kind, j - 1], (set_peer(j), p))
            else:
                own = acc
        for j in (1, 2, 3):
            remote(pick_out.at[kind, j - 1], pick_in.at[kind, j - 1],
                   set_send.at[1 + kind, j - 1], set_recv.at[1 + kind, j - 1], core).wait_recv()
            own = own + pick_in[kind, j - 1].astype(F32)
        return own.astype(BF16)

    for j in (1, 2, 3):
        src = set_peer(4 - j)
        remote(ints.at[src], ints.at[src], set_send.at[0, j - 1], set_recv.at[0, j - 1], core).wait_recv()

    def want_in(zz, j):
        return ints[set_peer(j), 0:1, 0:1] == zz * 4 + c

    taken = route(pages, 0, want_in)
    hid[pl.ds(pl.multiple_of(p * TOK + KEEP, 16), PAGE), :] = taken
    hg.first(2)

    z_step(2, yhi_w, 1, False)
    z_step(1, own_w, 2, True)
    z_step(2, yhi_w, 2, False)
    for item in (0, 1):
        for dz in (-1, 1):
            swap(item, dz)
    hg.second(0, True)
    hg.second(1, False)
    z_step(1, own_w, 3, True)
    z_step(2, yhi_w, 3, False)
    for item in (0, 1):
        for dz in (-2, 2, -3, 3):
            swap(item, dz)
    hg.second(2, True)
    z_step(1, own_w, 4, True)
    z_step(2, yhi_w, 4, False)
    for item in (0, 1):
        swap(item, 4)
    hg.third(0)
    hg.third(1)
    hg.third(2)
    for item in (0, 1):
        for dz in range(NZ):
            swap_wait(item, dz)
    for k in range(3):
        hg.last(k)
    for load in text_loads:
        load.wait()
    wout_load.wait()

    def rows_of(start, size=QB):
        return pl.ds(pl.multiple_of(start, 128), size)

    def project(t):
        rows = rows_of(t * QB)
        y = jnp.dot(hid[rows, :], wgt[...], preferred_element_type=F32).astype(BF16)
        for m in range(2):
            qry[m, rows, :] = y[:, m * DIM:(m + 1) * DIM]
            keys[m, rows, :] = y[:, (2 + m) * DIM:(3 + m) * DIM]
            vals[m, rows, :] = y[:, (4 + m) * DIM:(5 + m) * DIM]

    def attend(m, tok):
        q = qry[m, rows_of(tok), :]
        s = lax.dot_general(q, keys[m], (((1,), (1,)), ((), ())), preferred_element_type=F32)
        qseg = segment(tok + lax.broadcasted_iota(jnp.int32, (QB, 1), 0))
        s = jnp.where(qseg == kid[0:1, :], s, NEG_FILL)
        best = jnp.max(s, axis=1, keepdims=True)
        w = jnp.exp2((s - best) * EXP_SCALE)
        total_w = jnp.sum(w, axis=1, keepdims=True)
        o = jnp.dot(w.astype(BF16), vals[m], preferred_element_type=F32)
        return (o / total_w).astype(BF16)

    def gated(rows, start, heads):
        size = heads[0].shape[0]
        seg = segment(start + lax.broadcasted_iota(jnp.int32, (size, 1), 0))
        a = jnp.concatenate(heads, axis=1)

        def tile(n, carry):
            cols = pl.ds(pl.multiple_of(n * 512, 512), 512)
            proj = jnp.dot(a, wout[:, cols], preferred_element_type=F32)
            scale = gate[3:4, cols]
            for r in (2, 1, 0):
                scale = jnp.where(seg == r, gate[r:r + 1, cols], scale)
            hid[rows, cols] = (hid[rows, cols].astype(F32) + scale * proj).astype(BF16)
            return carry

        lax.fori_loop(0, 3, tile, 0)

    def item_of(k, ps):
        is_b = jnp.logical_or(k == 1, k == 3)
        tok_a = jnp.where(k == 0, 0, jnp.where(k == 2, 2, jnp.where(k == 4, 1, 3)))
        tok_b = (ps % 2) * 2 + jnp.where(k == 1, 0, 1)
        head = jnp.where(is_b, 8 + ps // 2, ps)
        return is_b.astype(jnp.int32), head, jnp.where(is_b, tok_b, tok_a) * QB

    def mix_at(k, ps):
        _, head, tok = item_of(k, ps)
        return mix.at[head, rows_of(tok), :]

    mg = Gather(mg_send, mg_recv, mix_at)

    def do_project(t, carry):
        project(t)
        return carry

    lax.fori_loop(0, SEQ // QB, do_project, 0)

    def step_one(k, carry):
        m, head, tok = item_of(k, p)
        mix[head, rows_of(tok), :] = attend(m, tok)
        mg.first(k)

        @pl.when(k >= 1)
        def _():
            mg.second(k - 1, (k - 1) % 2 == 0)

        @pl.when(k >= 2)
        def _():
            mg.third(k - 2)
        return carry

    lax.fori_loop(0, 6, step_one, 0)

    def widen(t):
        rows = rows_of(t * QB)
        gated(rows, t * QB, [mix[h, rows, :] for h in range(HEADS)])
        project(t)

    for k in range(3):
        hg.drain(k)
    mg.second(5, False)
    mg.third(4)
    mg.last(0)
    mg.last(1)
    widen(0)
    mg.third(5)
    mg.last(2)
    widen(2)
    mg.last(3)
    mg.last(4)
    widen(1)
    mg.last(5)
    widen(3)

    def piece(k, half, sent):
        m, head, tok = item_of(k, p)
        d = tok // TOK + half
        src = mine.at[k, pl.ds(half * TOK, TOK), :]

        if not sent:
            @pl.when(d == p)
            def _():
                pltpu.make_async_copy(src, fin.at[head], aa_recv.at[head]).start()

        @pl.when(d != p)
        def _():
            copy = remote(src, fin.at[head], aa_send.at[k, half], aa_recv.at[head], (g, d))
            if sent:
                copy.wait_send()
            else:
                copy.start()

    def step_two(k, carry):
        m, head, tok = item_of(k, p)
        mine[k] = attend(m, tok)
        for half in (0, 1):
            piece(k, half, False)
        return carry

    lax.fori_loop(0, 6, step_two, 0)

    def take_head(h, carry):
        remote(fin.at[h], fin.at[h], aa_send.at[0, 0], aa_recv.at[h], other).wait_recv()
        return carry

    lax.fori_loop(0, HEADS, take_head, 0)
    own_rows = rows_of(p * TOK, TOK)
    gated(own_rows, p * TOK, [fin[h] for h in range(HEADS)])
    back[z, :, 0:WIDTH] = hid[pl.ds(pl.multiple_of(p * TOK + KEEP, 16), PAGE), :]
    back[z, :, WIDTH:] = jnp.full((PAGE, TAG), inc[0, 0], jnp.int32).astype(F32).astype(BF16)
    z_first(3, back_at)
    out[0:KEEP, :] = hid[pl.ds(pl.multiple_of(p * TOK, 16), KEEP), :]
    for step in (1, 2, 3, 4):
        z_step(3, back_at, step, True)

    def want_back(zz, j):
        tag = back[zz, :, WIDTH:WIDTH + 1].astype(F32)
        return tag == set_peer(j).astype(F32)

    out[KEEP:TOK, :] = route(back, 1, want_back)

    for copy in pending:
        copy.wait_send()

    def drain(k, carry):
        mg.drain(k)
        for half in (0, 1):
            piece(k, half, True)
        return carry

    lax.fori_loop(0, 6, drain, 0)


def shards(latent, incoming, req_pages, text_len, gate_scale, text_keys, text_values, w_query, w_key, w_value, w_out):
    vm = pl.BlockSpec(memory_space=pltpu.VMEM)
    sm = pl.BlockSpec(memory_space=pltpu.SMEM)
    hb = pl.BlockSpec(memory_space=pl.ANY)
    dma = pltpu.SemaphoreType.DMA
    return pl.pallas_call(
        kernel,
        out_shape=jax.ShapeDtypeStruct((TOK, WIDTH), BF16),
        in_specs=[hb, sm, sm, sm, vm, hb, hb, hb, hb, hb, hb],
        out_specs=vm,
        scratch_shapes=[
            pltpu.VMEM((SEQ, WIDTH), BF16),
            pltpu.VMEM((WIDTH, 6 * DIM), BF16),
            pltpu.VMEM((WIDTH, WIDTH), BF16),
            pltpu.VMEM((HEADS, SEQ, DIM), BF16),
            pltpu.VMEM((2, KEYS, DIM), BF16),
            pltpu.VMEM((2, KEYS, DIM), BF16),
            pltpu.VMEM((2, SEQ, DIM), BF16),
            pltpu.VMEM((6, QB, DIM), BF16),
            pltpu.VMEM((HEADS, TOK, DIM), BF16),
            pltpu.VMEM((8, KEYS), jnp.int32),
            pltpu.VMEM((NZ, PAGE, WIDTH), BF16),
            pltpu.VMEM((NZ, PAGE, WIDTH + TAG), BF16),
            pltpu.VMEM((32, 8, 128), jnp.int32),
            pltpu.VMEM((2, 3, PAGE, WIDTH), BF16),
            pltpu.VMEM((2, 3, PAGE, WIDTH), BF16),
            dma((13,)),
            dma((4, 7)), dma((4, 7)),
            dma((2, NZ)), dma((2, NZ)),
            dma, dma,
            dma((3, 3)), dma((3, 3)),
            dma((3, 7)), dma((3, 7)),
            dma((6, 7)), dma((6, 7)),
            dma((6, 2)), dma((HEADS,)),
        ],
        compiler_params=pltpu.CompilerParams(
            collective_id=0, has_side_effects=True, vmem_limit_bytes=50 * 1024 * 1024),
        cost_estimate=pl.CostEstimate(flops=14_000_000_000, bytes_accessed=10_000_000, transcendentals=5_000_000),
    )(
        latent, incoming, req_pages, text_len, gate_scale[0],
        text_keys.reshape(REQS * TXT, WIDTH), text_values.reshape(REQS * TXT, WIDTH),
        w_query, w_key, w_value, w_out,
    )


def solution(mesh):
    in_specs = (
        P(("grp", "patch"), None),
        P("patch", "grp"),
        P("grp", None),
        P("grp", None),
        P("grp", None, None),
        P("grp", None, None, None),
        P("grp", None, None, None),
        P("grp", None),
        P("grp", None),
        P("grp", None),
        P(),
    )
    return jax.shard_map(
        shards, mesh=mesh, in_specs=in_specs, out_specs=P(("grp", "patch"), None), check_vma=False)
```

```python
import math

import jax
import jax.numpy as jnp
from jax import lax
from jax.experimental import pallas as pl
from jax.experimental.pallas import tpu as pltpu
from jax.sharding import PartitionSpec as P

MESH = pl.DeviceIdType.MESH
HEADS = 12
DIM = 128
WIDTH = 1536
PAGE = 16
REQS = 4
TXT = 128
TOK = 128
SEQ = 1024
KEEP = TOK - PAGE
NZ = 8
WROWS = 48
KEYS = SEQ + REQS * TXT
QB = 256
NEG_FILL = -1e30
TAG = 128
F32 = jnp.float32
BF16 = jnp.bfloat16
EXP_SCALE = math.log2(math.e) / math.sqrt(DIM)

PARTS = ((0, 64), (64, 48), (112, 16))


def kernel(
    lat, inc_h, req_pages_h, text_len_h, gate_h, text_k, text_v, w_q, w_k, w_v, w_o, out,
    hid, home, wgt, wout, mix, keys, vals, qry, mine, fin, kid,
    pages, back, ints, pick_out, pick_in, info, gate_w,
    inc, req_pages, text_len, gate, local_sem, z_send, z_recv, swap_send, swap_recv, yh_send, yh_recv,
    int_send, int_recv, set_send, set_recv, part_send, part_recv, text_send, text_recv,
    hg_send, hg_recv, mg_send, mg_recv, home_send, home_recv, aa_send, aa_recv,
):
    g = lax.axis_index("grp")
    p = lax.axis_index("patch")
    z, c = g // 4, g % 4
    yh, k = c // 2, c % 2
    x, yl = p % 4, p // 4
    same = k == yl
    apart = k != yl
    p4 = (p + 4) % 8
    core_g = g + 1 - 2 * k
    work_g = z * 4 + yh * 2 + yl

    right, left, far = (g, yl * 4 + (x + 1) % 4), (g, yl * 4 + (x + 3) % 4), (g, yl * 4 + (x + 2) % 4)
    up, down = ((g + 4) % 32, p), ((g + 28) % 32, p)
    yhi_g = z * 4 + (c + 2) % 4
    core, yhi, partner = (core_g, p), (yhi_g, p), (core_g, p4)

    def set_peer(j):
        return z * 4 + (c + j) % 4

    def zdev(dz, cc):
        return ((z + dz) % NZ) * 4 + cc

    head_a, head_b = 3 * x + 2 * k, 3 * x + 1

    def cols_of(head):
        return pl.ds(pl.multiple_of(head * DIM, DIM), DIM)

    def wrows(gg, first=0, count=3):
        return wgt.at[pl.ds(first, count), pl.ds(pl.multiple_of(gg * WROWS, 16), WROWS), :]

    loads = []
    my_rows = pl.ds(pl.multiple_of(g * WROWS, 16), WROWS)
    for n, w in enumerate((w_q, w_k, w_v)):
        for h in range(3):
            loads.append(pltpu.make_async_copy(
                w.at[:, cols_of(3 * x + h)], wgt.at[h, my_rows, pl.ds(n * DIM, DIM)], local_sem.at[3 * n + h]))
    my_hid = pl.ds(pl.multiple_of(p * TOK, TOK), KEEP)

    def text_copies(fn, heads):
        for n, (src, dst) in enumerate(((text_k, keys), (text_v, vals))):
            for m in range(2):
                fn(src.at[:, cols_of(heads[m])], dst.at[m, pl.ds(SEQ, REQS * TXT), :], 2 * n + m)

    def own_loads(fn):
        text_copies(lambda src, dst, n: fn(pltpu.make_async_copy(src, dst, local_sem.at[9 + n])), (head_a, head_b))
        fn(pltpu.make_async_copy(lat.at[pl.ds(0, KEEP), :], hid.at[my_hid, :], local_sem.at[13]))
        fn(pltpu.make_async_copy(gate_h, gate_w, local_sem.at[14]))

    wout_load = pltpu.make_async_copy(w_o, wout, local_sem.at[15])
    page_load = pltpu.make_async_copy(lat.at[pl.ds(KEEP, PAGE), :], pages.at[z], local_sem.at[16])
    small_loads = [
        pltpu.make_async_copy(src, dst, local_sem.at[17 + n])
        for n, (src, dst) in enumerate(((inc_h, inc), (req_pages_h, req_pages), (text_len_h, text_len), (gate_h, gate)))]
    page_load.start()
    for load in small_loads + loads:
        load.start()

    barrier = pltpu.get_barrier_semaphore()
    greeted = [up, down]
    plane = z * 4 + yh * 2
    for dk in range(2):
        for dp in range(8):
            if (dk, dp) != (0, 0):
                greeted.append((plane + (k + dk) % 2, (p + dp) % 8))
    other_plane = z * 4 + (1 - yh) * 2
    greeted += [(other_plane + dk, pp) for dk in range(2) for pp in (p, p4)]
    for peer in greeted:
        pl.semaphore_signal(barrier, inc=1, device_id=peer, device_id_type=MESH)
    pl.semaphore_wait(barrier, len(greeted))

    pending = []

    def remote(src, dst, send, recv, dev):
        return pltpu.make_async_remote_copy(
            src_ref=src, dst_ref=dst, send_sem=send, recv_sem=recv, device_id=dev, device_id_type=MESH)

    def go(*args):
        copy = remote(*args)
        copy.start()
        pending.append(copy)

    Z_FROM = (-1, -2, -3, 1, 2, 3, 4)

    def z_copy(item, at, slot, dz, dev):
        return remote(at(dz), at(dz), z_send.at[item, slot], z_recv.at[item, slot], dev)

    def z_go(item, at, slot, dz, dev):
        copy = z_copy(item, at, slot, dz, dev)
        copy.start()
        pending.append(copy)

    def z_wait(item, at, slot):
        z_copy(item, at, slot, Z_FROM[slot], up).wait_recv()

    def z_first(item, at):
        z_go(item, at, 0, 0, up)
        z_go(item, at, 3, 0, down)

    def z_step(item, at, step, last_up):
        if step == 4:
            z_wait(item, at, 6)
            return
        z_wait(item, at, step - 1)
        if step < 3:
            z_go(item, at, step, -step, up)
        elif last_up:
            z_go(item, at, 6, -3, up)
        z_wait(item, at, 2 + step)
        if step < 3:
            z_go(item, at, 3 + step, step, down)
        elif not last_up:
            z_go(item, at, 6, 3, down)

    def page_at(dz):
        return pages.at[(z + dz) % NZ]

    def back_at(dz):
        return back.at[(z + dz) % NZ]

    def own_w(dz):
        return wrows(zdev(dz, c))

    def yhi_w(dz):
        return wrows(zdev(dz, (c + 2) % 4))

    def swap(item, dz):
        ref = wrows(zdev(dz, (c + 2 * item) % 4), 1 - k, 2)
        go(ref, ref, swap_send.at[item, dz % NZ], swap_recv.at[item, dz % NZ], core)

    def swap_wait(item, dz):
        other_c = 2 * yh + 1 - k
        ref = wrows(zdev(dz, (other_c + 2 * item) % 4), k, 2)
        remote(ref, ref, swap_send.at[item, dz % NZ], swap_recv.at[item, dz % NZ], core).wait_recv()

    X_FROM = (3, 1, 2, 0, 3, 1, 2)

    class Gather:
        def __init__(self, send, recv, at):
            self.send, self.recv, self.at = send, recv, at

        def copy(self, n, slot, kk, dx, dev, src=None):
            ref = self.at(n, kk, (x + dx) % 4)
            return remote(ref if src is None else src, ref, self.send.at[n, slot], self.recv.at[n, slot], dev)

        def go(self, n, slot, dx, dev, src=None):
            self.copy(n, slot, k, dx, dev, src).start()

        def first(self, n, src=None):
            self.go(n, 0, 0, right, src)
            self.go(n, 1, 0, left, src)
            self.go(n, 3, 0, core, src)

        def direct(self, n):
            self.first(n)
            self.go(n, 2, 0, far)

        def wait(self, n, slot):
            self.copy(n, slot, k if slot < 3 else 1 - k, X_FROM[slot], core).wait_recv()

        def second(self, n, far_right):
            self.wait(n, 0)
            if far_right is True:
                self.go(n, 2, 3, right)
            self.go(n, 4, 3, core)
            self.wait(n, 1)
            if far_right is False:
                self.go(n, 2, 1, left)
            if far_right is not None and not isinstance(far_right, bool):
                @pl.when(far_right)
                def _():
                    self.go(n, 2, 3, right)

                @pl.when(jnp.logical_not(far_right))
                def _():
                    self.go(n, 2, 1, left)
            self.go(n, 5, 1, core)

        def third(self, n):
            self.wait(n, 2)
            self.go(n, 6, 2, core)

        def last(self, n):
            for slot in (3, 4, 5, 6):
                self.wait(n, slot)

        def drain(self, n):
            for slot in range(7):
                self.copy(n, slot, k, 0, core).wait_send()

    def hid_at(n, kk, xx):
        first, rows = PARTS[n]
        return hid.at[pl.ds(pl.multiple_of((kk * 4 + xx) * TOK + first, 16), rows), :]

    hg = Gather(hg_send, hg_recv, hid_at)

    def lat_part(n):
        return lat.at[pl.ds(*PARTS[n]), :]

    def part_copy(n):
        first, rows = PARTS[n]
        dst = hid.at[pl.ds(pl.multiple_of(p * TOK + first, 16), rows), :]
        return remote(lat_part(n), dst, part_send.at[n], part_recv.at[n], partner)

    def part_taken(n):
        return remote(lat_part(n), hid_at(n, k, x), part_send.at[n], part_recv.at[n], partner)

    page_load.wait()
    z_first(0, page_at)

    @pl.when(same)
    def _():
        for n in range(2):
            hg.first(n, lat_part(n))

    @pl.when(apart)
    def _():
        for n in range(2):
            part_copy(n).start()

    for load in loads:
        load.wait()
    z_first(1, own_w)
    go(wrows(g), wrows(g), yh_send, yh_recv, yhi)
    for load in small_loads:
        load.wait()
    ints[g] = jnp.full((8, 128), inc[0, 0], jnp.int32)
    for j in (1, 2, 3):
        go(ints.at[g], ints.at[g], int_send.at[j - 1], int_recv.at[j - 1], (set_peer(j), p))
    swap(0, 0)

    own_ends = []
    total = jnp.int32(0)
    for r in range(REQS):
        total = total + req_pages[0, r] * PAGE
        own_ends.append(total)

    def shared_copies(fn):
        fn(remote(info, info, text_send.at[4], text_recv.at[4], core))
        fn(remote(gate_h, gate_w, text_send.at[5], text_recv.at[5], core))
        text_copies(lambda src, dst, n: fn(remote(src, dst, text_send.at[n], text_recv.at[n], core)),
                    (3 * x + 2 - 2 * k, head_b))

    @pl.when(same)
    def _():
        for r in range(REQS):
            info[r] = jnp.full((8, 128), own_ends[r], jnp.int32)
            info[REQS + r] = jnp.full((8, 128), text_len[0, r], jnp.int32)
        own_loads(lambda copy: copy.start())
        shared_copies(lambda copy: copy.start())

    wout_load.start()

    def route_to(kind, cc):
        if kind:
            return (z * 4 + cc, p), c == cc
        here = yl == cc % 2
        return (z * 4 + jnp.where(here, cc, cc + 1 - 2 * (cc % 2)), jnp.where(here, p, p4)), jnp.logical_and(c == cc, same)

    def route_copy(kind, cc, slot, dev):
        return remote(pick_out.at[kind, cc], pick_in.at[kind, slot], set_send.at[kind, cc], set_recv.at[kind, slot], dev)

    def route_send(ring, kind, want):
        for cc in range(4):
            acc = jnp.zeros((PAGE, WIDTH), F32)
            for zz in range(NZ):
                acc = acc + jnp.where(want(zz, cc), ring[zz, :, 0:WIDTH].astype(F32), 0.0)
            dev, here = route_to(kind, cc)
            pick_out[kind, cc] = acc.astype(BF16)

            @pl.when(jnp.logical_not(here))
            def _():
                route_copy(kind, cc, c, dev).start()

            @pl.when(here)
            def _():
                pick_in[kind, cc] = acc.astype(BF16)

    def route_take(kind):
        for cc in range(4):
            @pl.when(jnp.logical_not(jnp.logical_and(c == cc, same) if not kind else c == cc))
            def _():
                route_copy(kind, cc, cc, core).wait_recv()
        return sum(pick_in[kind, cc].astype(F32) for cc in range(4)).astype(BF16)

    def route_drain(kind):
        for cc in range(4):
            dev, here = route_to(kind, cc)

            @pl.when(jnp.logical_not(here))
            def _():
                route_copy(kind, cc, c, dev).wait_send()

    def want_in(zz, cc):
        return ints[z * 4 + cc, 0:1, 0:1] == zz * 4 + c

    z_step(0, page_at, 1, True)
    z_step(1, own_w, 1, True)
    remote(wrows(yhi_g), wrows(yhi_g), yh_send, yh_recv, yhi).wait_recv()
    z_first(2, yhi_w)
    swap(1, 0)

    @pl.when(apart)
    def _():
        for n in range(2):
            part_taken(n).wait_recv()
            hg.first(n)

    z_step(0, page_at, 2, True)
    for dz in (-1, 1):
        swap(0, dz)
    z_step(1, own_w, 2, True)
    z_step(2, yhi_w, 1, False)
    z_step(0, page_at, 3, True)
    for dz in (-2, 2):
        swap(0, dz)
    for dz in (-1, 1):
        swap(1, dz)
    hg.second(0, True)
    hg.second(1, False)
    z_step(1, own_w, 3, True)
    z_step(2, yhi_w, 2, False)
    z_step(0, page_at, 4, True)
    for j in (1, 2, 3):
        src = set_peer(4 - j)
        remote(ints.at[src], ints.at[src], int_send.at[j - 1], int_recv.at[j - 1], core).wait_recv()
    route_send(pages, 0, want_in)
    z_step(2, yhi_w, 3, False)
    for dz in (-3, 3):
        swap(0, dz)
    for dz in (-2, 2, -3, 3):
        swap(1, dz)
    hid[pl.ds(pl.multiple_of((k * 4 + x) * TOK + KEEP, 16), PAGE), :] = route_take(0)
    hg.direct(2)
    hg.third(0)
    hg.third(1)
    z_step(1, own_w, 4, True)
    swap(0, 4)
    z_step(2, yhi_w, 4, False)
    swap(1, 4)

    @pl.when(same)
    def _():
        own_loads(lambda copy: copy.wait())

    @pl.when(apart)
    def _():
        shared_copies(lambda copy: copy.wait_recv())

    ends = [info[r, 0:1, 0:1] for r in range(REQS)]

    def segment(pos, bounds):
        seg = jnp.zeros(pos.shape, jnp.int32)
        for r in range(REQS):
            seg = seg + (pos >= bounds[r]).astype(jnp.int32)
        return seg

    kid[:, 0:SEQ] = segment(lax.broadcasted_iota(jnp.int32, (8, SEQ), 1), ends)
    for r in range(REQS):
        j = lax.broadcasted_iota(jnp.int32, (8, TXT), 1)
        kid[:, SEQ + r * TXT:SEQ + (r + 1) * TXT] = jnp.where(j < info[REQS + r, 0:1, 0:1], r, -1)

    wout_load.wait()
    hg.second(2, None)
    hg.third(2)
    for item in (0, 1):
        for dz in range(NZ):
            swap_wait(item, dz)
    for n in range(3):
        hg.last(n)

    def rows_of(start, size=QB):
        return pl.ds(pl.multiple_of(start, 128), size)

    def project(t):
        rows = rows_of(t * QB)
        w = jnp.concatenate([wgt[2 * k], wgt[1]], axis=1)
        y = jnp.dot(hid[rows, :], w, preferred_element_type=F32).astype(BF16)
        for m in range(2):
            qry[m, rows, :] = y[:, (3 * m) * DIM:(3 * m + 1) * DIM]
            keys[m, rows, :] = y[:, (3 * m + 1) * DIM:(3 * m + 2) * DIM]
            vals[m, rows, :] = y[:, (3 * m + 2) * DIM:(3 * m + 3) * DIM]

    def attend(m, tok):
        q = qry[m, rows_of(tok), :]
        s = lax.dot_general(q, keys[m], (((1,), (1,)), ((), ())), preferred_element_type=F32)
        qseg = segment(tok + lax.broadcasted_iota(jnp.int32, (QB, 1), 0), ends)
        s = jnp.where(qseg == kid[0:1, :], s, NEG_FILL)
        best = jnp.max(s, axis=1, keepdims=True)
        w = jnp.exp2((s - best) * EXP_SCALE)
        total_w = jnp.sum(w, axis=1, keepdims=True)
        o = jnp.dot(w.astype(BF16), vals[m], preferred_element_type=F32)
        return (o / total_w).astype(BF16)

    def gated(ref, rows, start, heads, bounds, gates):
        size = heads[0].shape[0]
        seg = segment(start + lax.broadcasted_iota(jnp.int32, (size, 1), 0), bounds)
        a = jnp.concatenate(heads, axis=1)

        def tile(n, carry):
            cols = pl.ds(pl.multiple_of(n * 512, 512), 512)
            proj = jnp.dot(a, wout[:, cols], preferred_element_type=F32)
            scale = gates[3:4, cols]
            for r in (2, 1, 0):
                scale = jnp.where(seg == r, gates[r:r + 1, cols], scale)
            ref[rows, cols] = (ref[rows, cols].astype(F32) + scale * proj).astype(BF16)
            return carry

        lax.fori_loop(0, 3, tile, 0)

    def item_of(n, kk, xx):
        is_b = jnp.logical_or(n == 1, n == 3)
        tok_a = jnp.where(n == 0, 0, jnp.where(n == 2, 2, jnp.where(n == 4, 1, 3)))
        tok_b = kk * 2 + jnp.where(n == 1, 0, 1)
        head = 3 * xx + jnp.where(is_b, 1, 2 * kk)
        return is_b.astype(jnp.int32), head, jnp.where(is_b, tok_b, tok_a) * QB

    def mix_at(n, kk, xx):
        _, head, tok = item_of(n, kk, xx)
        return mix.at[head, rows_of(tok), :]

    mg = Gather(mg_send, mg_recv, mix_at)

    def do_project(t, carry):
        project(t)
        return carry

    lax.fori_loop(0, SEQ // QB, do_project, 0)

    def step_one(n, carry):
        m, head, tok = item_of(n, k, x)
        mix[head, rows_of(tok), :] = attend(m, tok)
        mg.first(n)

        @pl.when(n >= 3)
        def _():
            mg.second(n - 3, (n - 3) % 2 == 0)
        return carry

    lax.fori_loop(0, 6, step_one, 0)

    def widen(t):
        rows = rows_of(t * QB)
        gated(hid, rows, t * QB, [mix[h, rows, :] for h in range(HEADS)], ends, gate_w)
        project(t)

    for n in range(3):
        hg.drain(n)
    mg.second(3, False)
    mg.second(4, True)
    mg.third(0)
    mg.third(1)
    mg.second(5, False)
    mg.last(0)
    mg.last(1)
    widen(0)
    mg.third(2)
    mg.third(3)
    mg.last(2)
    widen(2)
    mg.third(4)
    mg.third(5)
    mg.last(3)
    mg.last(4)
    widen(1)
    mg.last(5)
    widen(3)

    home_local = pltpu.make_async_copy(hid.at[rows_of(p * TOK, TOK), :], home, home_recv)
    home_copy = remote(hid.at[rows_of(p4 * TOK, TOK), :], home, home_send, home_recv, partner)

    @pl.when(same)
    def _():
        home_local.start()

    @pl.when(apart)
    def _():
        home_copy.start()

    def piece(n, half, sent):
        m, head, tok = item_of(n, k, x)
        d = tok // TOK + half
        src = mine.at[n, pl.ds(half * TOK, TOK), :]
        here = jnp.logical_and(same, d == p)

        if not sent:
            @pl.when(here)
            def _():
                pltpu.make_async_copy(src, fin.at[head], aa_recv.at[head]).start()

        @pl.when(jnp.logical_not(here))
        def _():
            copy = remote(src, fin.at[head], aa_send.at[n, half], aa_recv.at[head], (work_g, d))
            if sent:
                copy.wait_send()
            else:
                copy.start()

    def step_two(n, carry):
        m, head, tok = item_of(n, k, x)
        mine[n] = attend(m, tok)
        for half in (0, 1):
            piece(n, half, False)
        return carry

    lax.fori_loop(0, 6, step_two, 0)

    def take_head(h, carry):
        remote(fin.at[h], fin.at[h], aa_send.at[0, 0], aa_recv.at[h], core).wait_recv()
        return carry

    lax.fori_loop(0, HEADS, take_head, 0)
    home_copy.wait_recv()
    gated(home, pl.ds(0, TOK), p * TOK, [fin[h] for h in range(HEADS)], own_ends, gate)
    back[z, :, 0:WIDTH] = home[KEEP:TOK, :]
    back[z, :, WIDTH:] = jnp.full((PAGE, TAG), inc[0, 0], jnp.int32).astype(F32).astype(BF16)
    z_first(3, back_at)
    out[0:KEEP, :] = home[0:KEEP, :]
    for step in (1, 2, 3, 4):
        z_step(3, back_at, step, True)

    def want_back(zz, cc):
        return back[zz, :, WIDTH:WIDTH + 1].astype(F32) == (z * 4 + cc).astype(F32)

    route_send(back, 1, want_back)
    out[KEEP:TOK, :] = route_take(1)

    for copy in pending:
        copy.wait_send()
    route_drain(0)
    route_drain(1)

    @pl.when(same)
    def _():
        shared_copies(lambda copy: copy.wait_send())

    @pl.when(apart)
    def _():
        home_copy.wait_send()
        for n in range(2):
            part_copy(n).wait_send()

    def drain(n, carry):
        mg.drain(n)
        for half in (0, 1):
            piece(n, half, True)
        return carry

    lax.fori_loop(0, 6, drain, 0)


def shards(latent, incoming, req_pages, text_len, gate_scale, text_keys, text_values, w_query, w_key, w_value, w_out):
    vm = pl.BlockSpec(memory_space=pltpu.VMEM)
    hb = pl.BlockSpec(memory_space=pltpu.HBM)
    dma = pltpu.SemaphoreType.DMA
    return pl.pallas_call(
        kernel,
        out_shape=jax.ShapeDtypeStruct((TOK, WIDTH), BF16),
        in_specs=[hb] * 11,
        out_specs=vm,
        scratch_shapes=[
            pltpu.VMEM((SEQ, WIDTH), BF16),
            pltpu.VMEM((TOK, WIDTH), BF16),
            pltpu.VMEM((3, WIDTH, 3 * DIM), BF16),
            pltpu.VMEM((WIDTH, WIDTH), BF16),
            pltpu.VMEM((HEADS, SEQ, DIM), BF16),
            pltpu.VMEM((2, KEYS, DIM), BF16),
            pltpu.VMEM((2, KEYS, DIM), BF16),
            pltpu.VMEM((2, SEQ, DIM), BF16),
            pltpu.VMEM((6, QB, DIM), BF16),
            pltpu.VMEM((HEADS, TOK, DIM), BF16),
            pltpu.VMEM((8, KEYS), jnp.int32),
            pltpu.VMEM((NZ, PAGE, WIDTH), BF16),
            pltpu.VMEM((NZ, PAGE, WIDTH + TAG), BF16),
            pltpu.VMEM((32, 8, 128), jnp.int32),
            pltpu.VMEM((2, 4, PAGE, WIDTH), BF16),
            pltpu.VMEM((2, 4, PAGE, WIDTH), BF16),
            pltpu.VMEM((2 * REQS, 8, 128), jnp.int32),
            pltpu.VMEM((REQS, WIDTH), F32),
            pltpu.SMEM((1, 1), jnp.int32),
            pltpu.SMEM((1, REQS), jnp.int32),
            pltpu.SMEM((1, REQS), jnp.int32),
            pltpu.VMEM((REQS, WIDTH), F32),
            dma((21,)),
            dma((4, 7)), dma((4, 7)),
            dma((2, NZ)), dma((2, NZ)),
            dma, dma,
            dma((3,)), dma((3,)),
            dma((2, 4)), dma((2, 4)),
            dma((2,)), dma((2,)),
            dma((6,)), dma((6,)),
            dma((3, 7)), dma((3, 7)),
            dma((6, 7)), dma((6, 7)),
            dma, dma,
            dma((6, 2)), dma((HEADS,)),
        ],
        compiler_params=pltpu.CompilerParams(
            collective_id=0, has_side_effects=True, vmem_limit_bytes=56 * 1024 * 1024),
        cost_estimate=pl.CostEstimate(flops=14_000_000_000, bytes_accessed=10_000_000, transcendentals=5_000_000),
    )(
        latent, incoming, req_pages, text_len, gate_scale[0],
        text_keys.reshape(REQS * TXT, WIDTH), text_values.reshape(REQS * TXT, WIDTH),
        w_query, w_key, w_value, w_out,
    )


def solution(mesh):
    in_specs = (
        P(("grp", "patch"), None),
        P("patch", "grp"),
        P("grp", None),
        P("grp", None),
        P("grp", None, None),
        P("grp", None, None, None),
        P("grp", None, None, None),
        P("grp", None),
        P("grp", None),
        P("grp", None),
        P(),
    )
    return jax.shard_map(
        shards, mesh=mesh, in_specs=in_specs, out_specs=P(("grp", "patch"), None), check_vma=False)
```

```python
import math

import jax
import jax.numpy as jnp
from jax import lax
from jax.experimental import pallas as pl
from jax.experimental.pallas import tpu as pltpu
from jax.sharding import PartitionSpec as P

MESH = pl.DeviceIdType.MESH
HEADS = 12
DIM = 128
WIDTH = 1536
PAGE = 16
REQS = 4
TXT = 128
TOK = 128
SEQ = 1024
KEEP = TOK - PAGE
NZ = 8
WROWS = 48
BLOCKS = 10
KEYS = SEQ + REQS * TXT
QB = 256
NEG_FILL = -1e30
TAG = 128
F32 = jnp.float32
BF16 = jnp.bfloat16
EXP_SCALE = math.log2(math.e) / math.sqrt(DIM)

PARTS = ((0, 64), (64, 48), (112, 16))


def kernel(
    lat, inc_h, req_pages_h, text_len_h, gate_h, text_k, text_v, w_q, w_k, w_v, w_o, out,
    hid, home, wgt, wout, mix, keys, vals, qry, mine, fin, mine_page, fin_page, kid,
    pages, back, ints, pick_out, pick_in, info, gate_w,
    inc, req_pages, text_len, gate, local_sem, weight_sem, z_send, z_recv, swap_send, swap_recv, cross_send, cross_recv, pair_send, pair_recv,
    int_send, int_recv, set_send, set_recv, part_send, part_recv, text_send, text_recv,
    hg_send, hg_recv, mg_send, mg_recv, home_send, home_recv, aa_send, aa_recv, pa_send, pa_recv,
):
    g = lax.axis_index("grp")
    p = lax.axis_index("patch")
    z, c = g // 4, g % 4
    yh, k = c // 2, c % 2
    x, yl = p % 4, p // 4
    same = k == yl
    apart = k != yl
    p4 = (p + 4) % 8
    core_g = g + 1 - 2 * k
    work_g = z * 4 + yh * 2 + yl

    right, left, far = (g, yl * 4 + (x + 1) % 4), (g, yl * 4 + (x + 3) % 4), (g, yl * 4 + (x + 2) % 4)
    up, down = ((g + 4) % 32, p), ((g + 28) % 32, p)
    up2, down2 = ((g + 8) % 32, p), ((g + 24) % 32, p)
    yhi_g = z * 4 + (c + 2) % 4
    core, partner = (core_g, p), (core_g, p4)
    pair, cross = (g, p4), (yhi_g, p4)
    mine_first, other_first = 5 * yl, 5 - 5 * yl

    def set_peer(j):
        return z * 4 + (c + j) % 4

    def zdev(dz, cc):
        return ((z + dz) % NZ) * 4 + cc

    head_a, head_b = 3 * x + 2 * k, 3 * x + 1

    def cols_of(head):
        return pl.ds(pl.multiple_of(head * DIM, DIM), DIM)

    def wrows(gg, first=0, count=BLOCKS):
        return wgt.at[pl.ds(first, count), pl.ds(pl.multiple_of(gg * WROWS, 16), WROWS), :]

    my_rows = pl.ds(pl.multiple_of(g * WROWS, 16), WROWS)
    loads = []
    for b in range(BLOCKS):
        w = (w_q, w_k, w_v)[b % 3]
        loads.append(pltpu.make_async_copy(w.at[:, cols_of(3 * x + b // 3 % 3)], wgt.at[b, my_rows, :], weight_sem.at[b]))
    my_hid = pl.ds(pl.multiple_of(p * TOK, TOK), KEEP)

    def text_copies(fn, heads):
        for n, (src, dst) in enumerate(((text_k, keys), (text_v, vals))):
            for m in range(2):
                fn(src.at[:, cols_of(heads[m])], dst.at[m, pl.ds(SEQ, REQS * TXT), :], 2 * n + m)

    def own_loads(fn):
        text_copies(lambda src, dst, n: fn(pltpu.make_async_copy(src, dst, local_sem.at[n])), (head_a, head_b))
        fn(pltpu.make_async_copy(lat.at[pl.ds(0, KEEP), :], hid.at[my_hid, :], local_sem.at[4]))
        fn(pltpu.make_async_copy(gate_h, gate_w, local_sem.at[5]))

    wout_load = pltpu.make_async_copy(w_o, wout, local_sem.at[6])
    page_load = pltpu.make_async_copy(lat.at[pl.ds(KEEP, PAGE), :], pages.at[z], local_sem.at[7])
    small_loads = [
        pltpu.make_async_copy(src, dst, local_sem.at[8 + n])
        for n, (src, dst) in enumerate(((inc_h, inc), (req_pages_h, req_pages), (text_len_h, text_len), (gate_h, gate)))]
    page_load.start()
    for load in small_loads + loads:
        load.start()

    barrier = pltpu.get_barrier_semaphore()
    greeted = [up, down, up2, down2]
    plane = z * 4 + yh * 2
    for dk in range(2):
        for dp in range(8):
            if (dk, dp) != (0, 0):
                greeted.append((plane + (k + dk) % 2, (p + dp) % 8))
    other_plane = z * 4 + (1 - yh) * 2
    greeted += [(other_plane + dk, pp) for dk in range(2) for pp in (p, p4)]
    for peer in greeted:
        pl.semaphore_signal(barrier, inc=1, device_id=peer, device_id_type=MESH)
    pl.semaphore_wait(barrier, len(greeted))

    pending = []

    def remote(src, dst, send, recv, dev):
        return pltpu.make_async_remote_copy(
            src_ref=src, dst_ref=dst, send_sem=send, recv_sem=recv, device_id=dev, device_id_type=MESH)

    def go(*args):
        copy = remote(*args)
        copy.start()
        pending.append(copy)

    Z_FROM = (-1, -2, -3, 1, 2, 3, 4)

    def z_copy(item, at, slot, dz, dev):
        return remote(at(dz), at(dz), z_send.at[item, slot], z_recv.at[item, slot], dev)

    def z_go(item, at, slot, dz, dev):
        copy = z_copy(item, at, slot, dz, dev)
        copy.start()
        pending.append(copy)

    def z_wait(item, at, slot):
        z_copy(item, at, slot, Z_FROM[slot], up).wait_recv()

    def z_first(item, at):
        z_go(item, at, 0, 0, up)
        z_go(item, at, 3, 0, down)

    def z_step(item, at, step, last_up):
        if step == 4:
            z_wait(item, at, 6)
            return
        z_wait(item, at, step - 1)
        if step < 3:
            z_go(item, at, step, -step, up)
        elif last_up:
            z_go(item, at, 6, -3, up)
        z_wait(item, at, 2 + step)
        if step < 3:
            z_go(item, at, 3 + step, step, down)
        elif not last_up:
            z_go(item, at, 6, 3, down)

    def page_at(dz):
        return pages.at[(z + dz) % NZ]

    def back_at(dz):
        return back.at[(z + dz) % NZ]

    def own_w(dz):
        return wrows(zdev(dz, c), mine_first, 5)

    def yhi_w(dz):
        return wrows(zdev(dz, (c + 2) % 4), mine_first, 5)

    def y_go(dz):
        go(own_w(dz), own_w(dz), pair_send.at[dz % NZ], pair_recv.at[dz % NZ], pair)
        go(own_w(dz), own_w(dz), cross_send.at[dz % NZ], cross_recv.at[dz % NZ], cross)

    def y_take(dz):
        ref = wrows(zdev(dz, c), other_first, 5)
        remote(ref, ref, pair_send.at[dz % NZ], pair_recv.at[dz % NZ], pair).wait_recv()
        cross_take(dz)

    def cross_take(dz):
        ref = wrows(zdev(dz, (c + 2) % 4), other_first, 5)
        remote(ref, ref, cross_send.at[dz % NZ], cross_recv.at[dz % NZ], cross).wait_recv()

    def swap(item, dz):
        ref = wrows(zdev(dz, (c + 2 * item) % 4))
        go(ref, ref, swap_send.at[item, dz % NZ], swap_recv.at[item, dz % NZ], core)

    def swap_wait(item, dz):
        ref = wrows(zdev(dz, (2 * yh + 1 - k + 2 * item) % 4))
        remote(ref, ref, swap_send.at[item, dz % NZ], swap_recv.at[item, dz % NZ], core).wait_recv()

    X_FROM = (3, 1, 2, 0, 3, 1, 2)

    class Gather:
        def __init__(self, send, recv, at):
            self.send, self.recv, self.at = send, recv, at

        def copy(self, n, slot, kk, dx, dev, src=None):
            ref = self.at(n, kk, (x + dx) % 4)
            return remote(ref if src is None else src, ref, self.send.at[n, slot], self.recv.at[n, slot], dev)

        def go(self, n, slot, dx, dev, src=None):
            self.copy(n, slot, k, dx, dev, src).start()

        def first(self, n, src=None):
            self.go(n, 0, 0, right, src)
            self.go(n, 1, 0, left, src)
            self.go(n, 3, 0, core, src)

        def direct(self, n):
            self.first(n)
            self.go(n, 2, 0, far)

        def wait(self, n, slot):
            self.copy(n, slot, k if slot < 3 else 1 - k, X_FROM[slot], core).wait_recv()

        def second(self, n, far_right):
            self.wait(n, 0)
            if far_right is True:
                self.go(n, 2, 3, right)
            self.go(n, 4, 3, core)
            self.wait(n, 1)
            if far_right is False:
                self.go(n, 2, 1, left)
            if far_right is not None and not isinstance(far_right, bool):
                @pl.when(far_right)
                def _():
                    self.go(n, 2, 3, right)

                @pl.when(jnp.logical_not(far_right))
                def _():
                    self.go(n, 2, 1, left)
            self.go(n, 5, 1, core)

        def third(self, n):
            self.wait(n, 2)
            self.go(n, 6, 2, core)

        def last(self, n):
            for slot in (3, 4, 5, 6):
                self.wait(n, slot)

        def drain(self, n):
            for slot in range(7):
                self.copy(n, slot, k, 0, core).wait_send()

    def hid_at(n, kk, xx):
        first, rows = PARTS[n]
        return hid.at[pl.ds(pl.multiple_of((kk * 4 + xx) * TOK + first, 16), rows), :]

    hg = Gather(hg_send, hg_recv, hid_at)

    def lat_part(n):
        return lat.at[pl.ds(*PARTS[n]), :]

    def part_copy(n):
        first, rows = PARTS[n]
        dst = hid.at[pl.ds(pl.multiple_of(p * TOK + first, 16), rows), :]
        return remote(lat_part(n), dst, part_send.at[n], part_recv.at[n], partner)

    def part_taken(n):
        return remote(lat_part(n), hid_at(n, k, x), part_send.at[n], part_recv.at[n], partner)

    page_load.wait()
    z_first(0, page_at)

    @pl.when(same)
    def _():
        for n in range(2):
            hg.first(n, lat_part(n))

    @pl.when(apart)
    def _():
        for n in range(2):
            part_copy(n).start()

    for load in loads:
        load.wait()
    z_first(1, own_w)
    other_half = wrows(g, other_first, 5)
    go(other_half, other_half, cross_send.at[NZ], cross_recv.at[NZ], cross)
    go(own_w(0), own_w(0), cross_send.at[0], cross_recv.at[0], cross)
    for load in small_loads:
        load.wait()
    ints[g] = jnp.full((8, 128), inc[0, 0], jnp.int32)
    for j in (1, 2, 3):
        go(ints.at[g], ints.at[g], int_send.at[j - 1], int_recv.at[j - 1], (set_peer(j), p))
    swap(0, 0)

    own_ends = []
    total = jnp.int32(0)
    for r in range(REQS):
        total = total + req_pages[0, r] * PAGE
        own_ends.append(total)

    def shared_copies(fn):
        fn(remote(info, info, text_send.at[4], text_recv.at[4], core))
        fn(remote(gate_h, gate_w, text_send.at[5], text_recv.at[5], core))
        text_copies(lambda src, dst, n: fn(remote(src, dst, text_send.at[n], text_recv.at[n], core)),
                    (3 * x + 2 - 2 * k, head_b))

    @pl.when(same)
    def _():
        for r in range(REQS):
            info[r] = jnp.full((8, 128), own_ends[r], jnp.int32)
            info[REQS + r] = jnp.full((8, 128), text_len[0, r], jnp.int32)
        own_loads(lambda copy: copy.start())
        shared_copies(lambda copy: copy.start())

    wout_load.start()

    def route_to(kind, cc):
        if kind:
            return (z * 4 + cc, p), c == cc
        here = yl == cc % 2
        return (z * 4 + jnp.where(here, cc, cc + 1 - 2 * (cc % 2)), jnp.where(here, p, p4)), jnp.logical_and(c == cc, same)

    def route_copy(kind, cc, slot, dev):
        return remote(pick_out.at[kind, cc], pick_in.at[kind, slot], set_send.at[kind, cc], set_recv.at[kind, slot], dev)

    def route_send(ring, kind, want):
        for col in range(0, WIDTH, 512):
            accs = [jnp.zeros((PAGE, 512), F32)] * 4
            for zz in range(NZ):
                page = ring[zz, :, col:col + 512].astype(F32)
                accs = [jnp.where(want(zz, cc), page, accs[cc]) for cc in range(4)]
            for cc in range(4):
                pick_out[kind, cc, :, col:col + 512] = accs[cc].astype(BF16)
        for cc in range(4):
            dev, here = route_to(kind, cc)

            @pl.when(jnp.logical_not(here))
            def _():
                route_copy(kind, cc, c, dev).start()

            @pl.when(here)
            def _():
                pick_in[kind, cc] = pick_out[kind, cc]

    def route_take(kind):
        for cc in range(4):
            @pl.when(jnp.logical_not(jnp.logical_and(c == cc, same) if not kind else c == cc))
            def _():
                route_copy(kind, cc, cc, core).wait_recv()
        return sum(pick_in[kind, cc].astype(F32) for cc in range(4)).astype(BF16)

    def route_drain(kind):
        for cc in range(4):
            dev, here = route_to(kind, cc)

            @pl.when(jnp.logical_not(here))
            def _():
                route_copy(kind, cc, c, dev).wait_send()

    def want_in(zz, cc):
        return ints[z * 4 + cc, 0:1, 0:1] == zz * 4 + c

    z_step(0, page_at, 1, True)
    remote(yhi_w(0), yhi_w(0), cross_send.at[NZ], cross_recv.at[NZ], cross).wait_recv()
    z_first(2, yhi_w)
    z_step(1, own_w, 1, True)
    y_go(-1)
    y_go(1)

    @pl.when(apart)
    def _():
        for n in range(2):
            part_taken(n).wait_recv()
            hg.first(n)

    z_step(0, page_at, 2, True)
    z_step(2, yhi_w, 1, False)
    z_step(1, own_w, 2, True)
    y_go(-2)
    y_go(2)
    cross_take(0)
    swap(1, 0)
    z_step(0, page_at, 3, True)
    z_step(2, yhi_w, 2, False)
    z_step(1, own_w, 3, True)
    y_go(-3)
    y_go(3)
    hg.second(0, True)
    hg.second(1, False)
    z_step(0, page_at, 4, True)
    for j in (1, 2, 3):
        src = set_peer(4 - j)
        remote(ints.at[src], ints.at[src], int_send.at[j - 1], int_recv.at[j - 1], core).wait_recv()
    route_send(pages, 0, want_in)
    z_step(2, yhi_w, 3, False)
    z_step(1, own_w, 4, True)
    y_go(4)
    for dz in (-1, 1, -2, 2):
        y_take(dz)
        swap(0, dz)
        swap(1, dz)
    hg.third(0)
    hg.third(1)
    hid[pl.ds(pl.multiple_of((k * 4 + x) * TOK + KEEP, 16), PAGE), :] = route_take(0)
    hg.direct(2)
    for dz in (-3, 3):
        y_take(dz)
        swap(0, dz)
        swap(1, dz)
    z_step(2, yhi_w, 4, False)
    y_take(4)
    swap(0, 4)
    swap(1, 4)

    @pl.when(same)
    def _():
        own_loads(lambda copy: copy.wait())

    @pl.when(apart)
    def _():
        shared_copies(lambda copy: copy.wait_recv())

    ends = [info[r, 0:1, 0:1] for r in range(REQS)]

    def segment(pos, bounds):
        seg = jnp.zeros(pos.shape, jnp.int32)
        for r in range(REQS):
            seg = seg + (pos >= bounds[r]).astype(jnp.int32)
        return seg

    kid[:, 0:SEQ] = segment(lax.broadcasted_iota(jnp.int32, (8, SEQ), 1), ends)
    for r in range(REQS):
        j = lax.broadcasted_iota(jnp.int32, (8, TXT), 1)
        kid[:, SEQ + r * TXT:SEQ + (r + 1) * TXT] = jnp.where(j < info[REQS + r, 0:1, 0:1], r, -1)

    wout_load.wait()
    hg.second(2, None)
    hg.third(2)
    for item in (0, 1):
        for dz in range(NZ):
            swap_wait(item, dz)
    for n in range(3):
        hg.last(n)

    def rows_of(start, size=QB):
        return pl.ds(pl.multiple_of(start, 128), size)

    def project(t):
        rows = rows_of(t * QB)
        w = jnp.concatenate([wgt[6 * k + n] for n in range(3)] + [wgt[3 + n] for n in range(3)], axis=1)
        y = jnp.dot(hid[rows, :], w, preferred_element_type=F32).astype(BF16)
        for m in range(2):
            qry[m, rows, :] = y[:, (3 * m) * DIM:(3 * m + 1) * DIM]
            keys[m, rows, :] = y[:, (3 * m + 1) * DIM:(3 * m + 2) * DIM]
            vals[m, rows, :] = y[:, (3 * m + 2) * DIM:(3 * m + 3) * DIM]

    def attend(q, pos, m):
        s = lax.dot_general(q, keys[m], (((1,), (1,)), ((), ())), preferred_element_type=F32)
        s = jnp.where(segment(pos, ends) == kid[0:1, :], s, NEG_FILL)
        best = jnp.max(s, axis=1, keepdims=True)
        w = jnp.exp2((s - best) * EXP_SCALE)
        total_w = jnp.sum(w, axis=1, keepdims=True)
        o = jnp.dot(w.astype(BF16), vals[m], preferred_element_type=F32)
        return (o / total_w).astype(BF16)

    def gated(ref, rows, start, heads, bounds, gates):
        size = heads[0].shape[0]
        seg = segment(start + lax.broadcasted_iota(jnp.int32, (size, 1), 0), bounds)
        a = jnp.concatenate(heads, axis=1)

        def tile(n, carry):
            cols = pl.ds(pl.multiple_of(n * 512, 512), 512)
            proj = jnp.dot(a, wout[:, cols], preferred_element_type=F32)
            scale = gates[3:4, cols]
            for r in (2, 1, 0):
                scale = jnp.where(seg == r, gates[r:r + 1, cols], scale)
            ref[rows, cols] = (ref[rows, cols].astype(F32) + scale * proj).astype(BF16)
            return carry

        lax.fori_loop(0, 3, tile, 0)

    def item_of(n, kk, xx):
        is_b = jnp.logical_or(n == 1, n == 3)
        tok_a = jnp.where(n == 0, 0, jnp.where(n == 2, 2, jnp.where(n == 4, 1, 3)))
        tok_b = kk * 2 + jnp.where(n == 1, 0, 1)
        head = 3 * xx + jnp.where(is_b, 1, 2 * kk)
        return is_b.astype(jnp.int32), head, jnp.where(is_b, tok_b, tok_a) * QB

    def mix_at(n, kk, xx):
        _, head, tok = item_of(n, kk, xx)
        return mix.at[head, rows_of(tok), :]

    mg = Gather(mg_send, mg_recv, mix_at)

    def do_project(t, carry):
        project(t)
        return carry

    lax.fori_loop(0, SEQ // QB, do_project, 0)

    def step_one(n, carry):
        m, head, tok = item_of(n, k, x)
        pos = tok + lax.broadcasted_iota(jnp.int32, (QB, 1), 0)
        mix[head, rows_of(tok), :] = attend(qry[m, rows_of(tok), :], pos, m)
        mg.first(n)

        @pl.when(n >= 3)
        def _():
            mg.second(n - 3, (n - 3) % 2 == 0)
        return carry

    lax.fori_loop(0, 6, step_one, 0)

    def widen(t):
        rows = rows_of(t * QB)
        gated(hid, rows, t * QB, [mix[h, rows, :] for h in range(HEADS)], ends, gate_w)
        project(t)

    for n in range(3):
        hg.drain(n)
    mg.second(3, False)
    mg.second(4, True)
    mg.third(0)
    mg.third(1)
    mg.second(5, False)
    mg.last(0)
    mg.last(1)
    widen(0)
    mg.third(2)
    mg.third(3)
    mg.last(2)
    widen(2)
    mg.third(4)
    mg.third(5)
    mg.last(3)
    mg.last(4)
    widen(1)
    mg.last(5)
    widen(3)

    home_local = pltpu.make_async_copy(hid.at[rows_of(p * TOK, TOK), :], home, home_recv)
    home_copy = remote(hid.at[rows_of(p4 * TOK, TOK), :], home, home_send, home_recv, partner)

    @pl.when(same)
    def _():
        home_local.start()

    @pl.when(apart)
    def _():
        home_copy.start()

    def send_home(src, dst, send, recv, d, sent):
        here = jnp.logical_and(same, d == p)

        if not sent:
            @pl.when(here)
            def _():
                pltpu.make_async_copy(src, dst, recv).start()

        @pl.when(jnp.logical_not(here))
        def _():
            copy = remote(src, dst, send, recv, (work_g, d))
            if sent:
                copy.wait_send()
            else:
                copy.start()

    def page_piece(n, sent):
        head = 3 * x + jnp.where(n < 8, 2 * k, 1)
        d = jnp.where(n < 8, n, k * 4 + n - 8)
        send_home(mine_page.at[n], fin_page.at[head], pa_send.at[n], pa_recv.at[head], d, sent)

    def piece(n, half, sent):
        m = (n >= 4).astype(jnp.int32)
        head = 3 * x + jnp.where(n < 4, 2 * k, 1)
        d = jnp.where(n < 4, 2 * n, k * 4 + 2 * (n - 4)) + half
        send_home(mine.at[n, half], fin.at[head], aa_send.at[n, half], aa_recv.at[head], d, sent)
        return m, d

    def block_pos(rows, block, first):
        i = lax.broadcasted_iota(jnp.int32, (rows, 1), 0)
        return first + i + (i // block) * (TOK - block)

    for m, count, first in ((0, 8, 0), (1, 4, k * 4)):
        q = jnp.concatenate(
            [qry[m, pl.ds(pl.multiple_of((first + j) * TOK + KEEP, 16), PAGE), :] for j in range(count)], axis=0)
        o = attend(q, block_pos(count * PAGE, PAGE, first * TOK + KEEP), m)
        for j in range(count):
            mine_page[8 * m + j] = o[j * PAGE:(j + 1) * PAGE]

    def send_page(n, carry):
        page_piece(n, False)
        return carry

    lax.fori_loop(0, 12, send_page, 0)

    def step_two(n, carry):
        m = (n >= 4).astype(jnp.int32)
        d = jnp.where(n < 4, 2 * n, k * 4 + 2 * (n - 4))
        q = jnp.concatenate(
            [qry[m, pl.ds(pl.multiple_of((d + j) * TOK, 128), KEEP), :] for j in range(2)], axis=0)
        o = attend(q, block_pos(2 * KEEP, KEEP, d * TOK), m)
        for half in (0, 1):
            mine[n, half] = o[half * KEEP:(half + 1) * KEEP]
        for half in (0, 1):
            piece(n, half, False)
        return carry

    def take_heads(ref, recv):
        def take(h, carry):
            remote(ref.at[h], ref.at[h], aa_send.at[0, 0], recv.at[h], core).wait_recv()
            return carry

        lax.fori_loop(0, HEADS, take, 0)

    lax.fori_loop(0, 2, step_two, 0)
    take_heads(fin_page, pa_recv)
    home_copy.wait_recv()
    gated(home, pl.ds(KEEP, PAGE), p * TOK + KEEP, [fin_page[h] for h in range(HEADS)], own_ends, gate)
    back[z, :, 0:WIDTH] = home[KEEP:TOK, :]
    back[z, :, WIDTH:] = jnp.full((PAGE, TAG), inc[0, 0], jnp.int32).astype(F32).astype(BF16)

    def half_at(dz, first, count):
        return back.at[(z + dz) % NZ, :, pl.ds(first, count)]

    HALVES = ((6, 0, WIDTH // 2), (7, WIDTH // 2, WIDTH // 2 + TAG))

    def half_copy(n, dz, dev):
        slot, first, count = HALVES[n]
        ref = half_at(dz, first, count)
        return remote(ref, ref, z_send.at[3, slot], z_recv.at[3, slot], dev)

    def half_go(n, dz, dev):
        copy = half_copy(n, dz, dev)
        copy.start()
        pending.append(copy)

    z_go(3, back_at, 1, 0, up2)
    z_go(3, back_at, 4, 0, down2)
    z_first(3, back_at)
    lax.fori_loop(2, 6, step_two, 0)
    z_wait(3, back_at, 1)
    half_go(0, -2, up2)
    z_go(3, back_at, 2, -2, up)
    z_wait(3, back_at, 4)
    half_go(1, 2, down2)
    z_go(3, back_at, 5, 2, down)
    take_heads(fin, aa_recv)
    gated(home, pl.ds(0, KEEP), p * TOK, [fin[h] for h in range(HEADS)], own_ends, gate)
    out[0:KEEP, :] = home[0:KEEP, :]
    for slot in (0, 3, 2, 5):
        z_wait(3, back_at, slot)
    for n in (0, 1):
        half_copy(n, 4, up).wait_recv()

    def want_back(zz, cc):
        return back[zz, :, WIDTH:WIDTH + 1].astype(F32) == (z * 4 + cc).astype(F32)

    route_send(back, 1, want_back)
    out[KEEP:TOK, :] = route_take(1)

    for copy in pending:
        copy.wait_send()
    route_drain(0)
    route_drain(1)

    @pl.when(same)
    def _():
        shared_copies(lambda copy: copy.wait_send())

    @pl.when(apart)
    def _():
        home_copy.wait_send()
        for n in range(2):
            part_copy(n).wait_send()

    def drain(n, carry):
        mg.drain(n)
        for half in (0, 1):
            piece(n, half, True)
            page_piece(2 * n + half, True)
        return carry

    lax.fori_loop(0, 6, drain, 0)


def shards(latent, incoming, req_pages, text_len, gate_scale, text_keys, text_values, w_query, w_key, w_value, w_out):
    vm = pl.BlockSpec(memory_space=pltpu.VMEM)
    hb = pl.BlockSpec(memory_space=pltpu.HBM)
    dma = pltpu.SemaphoreType.DMA
    return pl.pallas_call(
        kernel,
        out_shape=jax.ShapeDtypeStruct((TOK, WIDTH), BF16),
        in_specs=[hb] * 11,
        out_specs=vm,
        scratch_shapes=[
            pltpu.VMEM((SEQ, WIDTH), BF16),
            pltpu.VMEM((TOK, WIDTH), BF16),
            pltpu.VMEM((BLOCKS, WIDTH, DIM), BF16),
            pltpu.VMEM((WIDTH, WIDTH), BF16),
            pltpu.VMEM((HEADS, SEQ, DIM), BF16),
            pltpu.VMEM((2, KEYS, DIM), BF16),
            pltpu.VMEM((2, KEYS, DIM), BF16),
            pltpu.VMEM((2, SEQ, DIM), BF16),
            pltpu.VMEM((6, 2, KEEP, DIM), BF16),
            pltpu.VMEM((HEADS, KEEP, DIM), BF16),
            pltpu.VMEM((12, PAGE, DIM), BF16),
            pltpu.VMEM((HEADS, PAGE, DIM), BF16),
            pltpu.VMEM((8, KEYS), jnp.int32),
            pltpu.VMEM((NZ, PAGE, WIDTH), BF16),
            pltpu.VMEM((NZ, PAGE, WIDTH + TAG), BF16),
            pltpu.VMEM((32, 8, 128), jnp.int32),
            pltpu.VMEM((2, 4, PAGE, WIDTH), BF16),
            pltpu.VMEM((2, 4, PAGE, WIDTH), BF16),
            pltpu.VMEM((2 * REQS, 8, 128), jnp.int32),
            pltpu.VMEM((REQS, WIDTH), F32),
            pltpu.SMEM((1, 1), jnp.int32),
            pltpu.SMEM((1, REQS), jnp.int32),
            pltpu.SMEM((1, REQS), jnp.int32),
            pltpu.VMEM((REQS, WIDTH), F32),
            dma((12,)), dma((BLOCKS,)),
            dma((4, 8)), dma((4, 8)),
            dma((2, NZ)), dma((2, NZ)),
            dma((NZ + 1,)), dma((NZ + 1,)),
            dma((NZ,)), dma((NZ,)),
            dma((3,)), dma((3,)),
            dma((2, 4)), dma((2, 4)),
            dma((2,)), dma((2,)),
            dma((6,)), dma((6,)),
            dma((3, 7)), dma((3, 7)),
            dma((6, 7)), dma((6, 7)),
            dma, dma,
            dma((6, 2)), dma((HEADS,)),
            dma((12,)), dma((HEADS,)),
        ],
        compiler_params=pltpu.CompilerParams(
            collective_id=0, has_side_effects=True, vmem_limit_bytes=56 * 1024 * 1024),
        cost_estimate=pl.CostEstimate(flops=14_000_000_000, bytes_accessed=10_000_000, transcendentals=5_000_000),
    )(
        latent, incoming, req_pages, text_len, gate_scale[0],
        text_keys.reshape(REQS * TXT, WIDTH), text_values.reshape(REQS * TXT, WIDTH),
        w_query, w_key, w_value, w_out,
    )


def solution(mesh):
    in_specs = (
        P(("grp", "patch"), None),
        P("patch", "grp"),
        P("grp", None),
        P("grp", None),
        P("grp", None, None),
        P("grp", None, None, None),
        P("grp", None, None, None),
        P("grp", None),
        P("grp", None),
        P("grp", None),
        P(),
    )
    return jax.shard_map(
        shards, mesh=mesh, in_specs=in_specs, out_specs=P(("grp", "patch"), None), check_vma=False)
```

```python
import math

import jax
import jax.numpy as jnp
from jax import lax
from jax.experimental import pallas as pl
from jax.experimental.pallas import tpu as pltpu
from jax.sharding import PartitionSpec as P

MESH = pl.DeviceIdType.MESH
HEADS = 12
DIM = 128
WIDTH = 1536
PAGE = 16
REQS = 4
TXT = 128
TOK = 128
SEQ = 1024
KEEP = TOK - PAGE
NZ = 8
WROWS = 48
BLOCKS = 10
KEYS = SEQ + REQS * TXT
QB = 256
NEG_FILL = -1e30
TAG = 128
F32 = jnp.float32
BF16 = jnp.bfloat16
EXP_SCALE = math.log2(math.e) / math.sqrt(DIM)

PARTS = ((0, 64), (64, 48), (112, 16))


def kernel(
    lat, inc_h, req_pages_h, text_len_h, gate_h, text_k, text_v, w_q, w_k, w_v, w_o, out,
    hid, home, wgt, wout, mix, keys, vals, qry, mine, fin, mine_page, fin_page, kid,
    pages, back, ints, pick_out, pick_in, info, gate_w,
    inc, req_pages, text_len, gate, local_sem, weight_sem, z_send, z_recv, swap_send, swap_recv, cross_send, cross_recv, pair_send, pair_recv,
    int_send, int_recv, set_send, set_recv, part_send, part_recv, text_send, text_recv,
    hg_send, hg_recv, mg_send, mg_recv, home_send, home_recv, aa_send, aa_recv, pa_send, pa_recv,
):
    g = lax.axis_index("grp")
    p = lax.axis_index("patch")
    z, c = g // 4, g % 4
    yh, k = c // 2, c % 2
    x, yl = p % 4, p // 4
    same = k == yl
    apart = k != yl
    p4 = (p + 4) % 8
    core_g = g + 1 - 2 * k
    work_g = z * 4 + yh * 2 + yl

    right, left, far = (g, yl * 4 + (x + 1) % 4), (g, yl * 4 + (x + 3) % 4), (g, yl * 4 + (x + 2) % 4)
    up, down = ((g + 4) % 32, p), ((g + 28) % 32, p)
    up2, down2 = ((g + 8) % 32, p), ((g + 24) % 32, p)
    yhi_g = z * 4 + (c + 2) % 4
    core, partner = (core_g, p), (core_g, p4)
    pair, cross = (g, p4), (yhi_g, p4)
    mine_first, other_first = 5 * yl, 5 - 5 * yl

    def set_peer(j):
        return z * 4 + (c + j) % 4

    def zdev(dz, cc):
        return ((z + dz) % NZ) * 4 + cc

    head_a, head_b = 3 * x + 2 * k, 3 * x + 1

    def cols_of(head):
        return pl.ds(pl.multiple_of(head * DIM, DIM), DIM)

    def wrows(gg, first=0, count=BLOCKS):
        return wgt.at[pl.ds(first, count), pl.ds(pl.multiple_of(gg * WROWS, 16), WROWS), :]

    my_rows = pl.ds(pl.multiple_of(g * WROWS, 16), WROWS)
    loads = []
    for b in range(BLOCKS):
        w = (w_q, w_k, w_v)[b % 3]
        loads.append(pltpu.make_async_copy(w.at[:, cols_of(3 * x + b // 3 % 3)], wgt.at[b, my_rows, :], weight_sem.at[b]))
    my_hid = pl.ds(pl.multiple_of(p * TOK, TOK), KEEP)

    def text_copies(fn, heads):
        for n, (src, dst) in enumerate(((text_k, keys), (text_v, vals))):
            for m in range(2):
                fn(src.at[:, cols_of(heads[m])], dst.at[m, pl.ds(SEQ, REQS * TXT), :], 2 * n + m)

    def own_loads(fn):
        text_copies(lambda src, dst, n: fn(pltpu.make_async_copy(src, dst, local_sem.at[n])), (head_a, head_b))
        fn(pltpu.make_async_copy(lat.at[pl.ds(0, KEEP), :], hid.at[my_hid, :], local_sem.at[4]))
        fn(pltpu.make_async_copy(gate_h, gate_w, local_sem.at[5]))

    wout_load = pltpu.make_async_copy(w_o, wout, local_sem.at[6])
    page_load = pltpu.make_async_copy(lat.at[pl.ds(KEEP, PAGE), :], pages.at[z], local_sem.at[7])
    small_loads = [
        pltpu.make_async_copy(src, dst, local_sem.at[8 + n])
        for n, (src, dst) in enumerate(((inc_h, inc), (req_pages_h, req_pages), (text_len_h, text_len), (gate_h, gate)))]
    page_load.start()
    for load in small_loads + loads:
        load.start()

    barrier = pltpu.get_barrier_semaphore()
    greeted = [up, down, up2, down2]
    plane = z * 4 + yh * 2
    for dk in range(2):
        for dp in range(8):
            if (dk, dp) != (0, 0):
                greeted.append((plane + (k + dk) % 2, (p + dp) % 8))
    other_plane = z * 4 + (1 - yh) * 2
    greeted += [(other_plane + dk, pp) for dk in range(2) for pp in (p, p4)]
    for peer in greeted:
        pl.semaphore_signal(barrier, inc=1, device_id=peer, device_id_type=MESH)
    pl.semaphore_wait(barrier, len(greeted))

    pending = []

    def remote(src, dst, send, recv, dev):
        return pltpu.make_async_remote_copy(
            src_ref=src, dst_ref=dst, send_sem=send, recv_sem=recv, device_id=dev, device_id_type=MESH)

    def go(*args):
        copy = remote(*args)
        copy.start()
        pending.append(copy)

    Z_FROM = (-1, -2, -3, 1, 2, 3, 4)

    def z_copy(item, at, slot, dz, dev):
        return remote(at(dz), at(dz), z_send.at[item, slot], z_recv.at[item, slot], dev)

    def z_go(item, at, slot, dz, dev):
        copy = z_copy(item, at, slot, dz, dev)
        copy.start()
        pending.append(copy)

    def z_wait(item, at, slot):
        z_copy(item, at, slot, Z_FROM[slot], up).wait_recv()

    def z_first(item, at):
        z_go(item, at, 0, 0, up)
        z_go(item, at, 3, 0, down)

    def z_step(item, at, step, last_up):
        if step == 4:
            z_wait(item, at, 6)
            return
        z_wait(item, at, step - 1)
        if step < 3:
            z_go(item, at, step, -step, up)
        elif last_up:
            z_go(item, at, 6, -3, up)
        z_wait(item, at, 2 + step)
        if step < 3:
            z_go(item, at, 3 + step, step, down)
        elif not last_up:
            z_go(item, at, 6, 3, down)

    def two_copy(item, slot, dz, dev, src=None):
        ring, first, count = pages if item == 0 else back, 0, WIDTH + (TAG if item else 0)
        if slot == 6:
            count = WIDTH // 2
        if slot == 7:
            first, count = WIDTH // 2, count - WIDTH // 2
        ref = ring.at[(z + dz) % NZ, :, pl.ds(first, count)]
        return remote(ref if src is None else src, ref, z_send.at[item, slot], z_recv.at[item, slot], dev)

    def two_go(item, slot, dz, dev, src=None):
        copy = two_copy(item, slot, dz, dev, src)
        copy.start()
        pending.append(copy)

    def two_first(item, src=None):
        two_go(item, 1, 0, up2, src)
        two_go(item, 4, 0, down2, src)
        two_go(item, 0, 0, up, src)
        two_go(item, 3, 0, down, src)

    def two_second(item):
        two_copy(item, 1, -2, up).wait_recv()
        two_go(item, 6, -2, up2)
        two_go(item, 2, -2, up)
        two_copy(item, 4, 2, up).wait_recv()
        two_go(item, 7, 2, down2)
        two_go(item, 5, 2, down)

    def two_last(item):
        for slot, dz in ((0, -1), (3, 1), (2, -3), (5, 3), (6, 4), (7, 4)):
            two_copy(item, slot, dz, up).wait_recv()

    def own_w(dz):
        return wrows(zdev(dz, c), mine_first, 5)

    def yhi_w(dz):
        return wrows(zdev(dz, (c + 2) % 4), mine_first, 5)

    def y_go(dz):
        go(own_w(dz), own_w(dz), pair_send.at[dz % NZ], pair_recv.at[dz % NZ], pair)
        go(own_w(dz), own_w(dz), cross_send.at[dz % NZ], cross_recv.at[dz % NZ], cross)

    def y_take(dz):
        ref = wrows(zdev(dz, c), other_first, 5)
        remote(ref, ref, pair_send.at[dz % NZ], pair_recv.at[dz % NZ], pair).wait_recv()
        cross_take(dz)

    def cross_take(dz):
        ref = wrows(zdev(dz, (c + 2) % 4), other_first, 5)
        remote(ref, ref, cross_send.at[dz % NZ], cross_recv.at[dz % NZ], cross).wait_recv()

    def swap(item, dz):
        ref = wrows(zdev(dz, (c + 2 * item) % 4))
        go(ref, ref, swap_send.at[item, dz % NZ], swap_recv.at[item, dz % NZ], core)

    def swap_wait(item, dz):
        ref = wrows(zdev(dz, (2 * yh + 1 - k + 2 * item) % 4))
        remote(ref, ref, swap_send.at[item, dz % NZ], swap_recv.at[item, dz % NZ], core).wait_recv()

    X_FROM = (3, 1, 2, 0, 3, 1, 2)

    class Gather:
        def __init__(self, send, recv, at):
            self.send, self.recv, self.at = send, recv, at

        def copy(self, n, slot, kk, dx, dev, src=None):
            ref = self.at(n, kk, (x + dx) % 4)
            return remote(ref if src is None else src, ref, self.send.at[n, slot], self.recv.at[n, slot], dev)

        def go(self, n, slot, dx, dev, src=None):
            self.copy(n, slot, k, dx, dev, src).start()

        def first(self, n, src=None):
            self.go(n, 0, 0, right, src)
            self.go(n, 1, 0, left, src)
            self.go(n, 3, 0, core, src)

        def direct(self, n):
            self.first(n)
            self.go(n, 2, 0, far)

        def wait(self, n, slot):
            self.copy(n, slot, k if slot < 3 else 1 - k, X_FROM[slot], core).wait_recv()

        def second(self, n, far_right):
            self.wait(n, 0)
            if far_right is True:
                self.go(n, 2, 3, right)
            self.go(n, 4, 3, core)
            self.wait(n, 1)
            if far_right is False:
                self.go(n, 2, 1, left)
            if far_right is not None and not isinstance(far_right, bool):
                @pl.when(far_right)
                def _():
                    self.go(n, 2, 3, right)

                @pl.when(jnp.logical_not(far_right))
                def _():
                    self.go(n, 2, 1, left)
            self.go(n, 5, 1, core)

        def third(self, n):
            self.wait(n, 2)
            self.go(n, 6, 2, core)

        def last(self, n):
            for slot in (3, 4, 5, 6):
                self.wait(n, slot)

        def drain(self, n):
            for slot in range(7):
                self.copy(n, slot, k, 0, core).wait_send()

    def hid_at(n, kk, xx):
        first, rows = PARTS[n]
        return hid.at[pl.ds(pl.multiple_of((kk * 4 + xx) * TOK + first, 16), rows), :]

    hg = Gather(hg_send, hg_recv, hid_at)

    def lat_part(n):
        return lat.at[pl.ds(*PARTS[n]), :]

    def part_copy(n):
        first, rows = PARTS[n]
        dst = hid.at[pl.ds(pl.multiple_of(p * TOK + first, 16), rows), :]
        return remote(lat_part(n), dst, part_send.at[n], part_recv.at[n], partner)

    def part_taken(n):
        return remote(lat_part(n), hid_at(n, k, x), part_send.at[n], part_recv.at[n], partner)

    two_first(0, lat.at[pl.ds(KEEP, PAGE), :])

    @pl.when(same)
    def _():
        for n in range(2):
            hg.first(n, lat_part(n))

    @pl.when(apart)
    def _():
        for n in range(2):
            part_copy(n).start()

    for load in loads:
        load.wait()
    z_first(1, own_w)
    other_half = wrows(g, other_first, 5)
    go(other_half, other_half, cross_send.at[NZ], cross_recv.at[NZ], cross)
    go(own_w(0), own_w(0), cross_send.at[0], cross_recv.at[0], cross)
    for load in small_loads:
        load.wait()
    ints[g] = jnp.full((8, 128), inc[0, 0], jnp.int32)
    for j in (1, 2, 3):
        go(ints.at[g], ints.at[g], int_send.at[j - 1], int_recv.at[j - 1], (set_peer(j), p))
    swap(0, 0)

    own_ends = []
    total = jnp.int32(0)
    for r in range(REQS):
        total = total + req_pages[0, r] * PAGE
        own_ends.append(total)

    def shared_copies(fn):
        fn(remote(info, info, text_send.at[4], text_recv.at[4], core))
        fn(remote(gate_h, gate_w, text_send.at[5], text_recv.at[5], core))
        text_copies(lambda src, dst, n: fn(remote(src, dst, text_send.at[n], text_recv.at[n], core)),
                    (3 * x + 2 - 2 * k, head_b))

    @pl.when(same)
    def _():
        for r in range(REQS):
            info[r] = jnp.full((8, 128), own_ends[r], jnp.int32)
            info[REQS + r] = jnp.full((8, 128), text_len[0, r], jnp.int32)
        own_loads(lambda copy: copy.start())
        shared_copies(lambda copy: copy.start())

    wout_load.start()

    def route_to(kind, cc):
        if kind:
            return (z * 4 + cc, p), c == cc
        here = yl == cc % 2
        return (z * 4 + jnp.where(here, cc, cc + 1 - 2 * (cc % 2)), jnp.where(here, p, p4)), jnp.logical_and(c == cc, same)

    def route_copy(kind, cc, slot, dev):
        return remote(pick_out.at[kind, cc], pick_in.at[kind, slot], set_send.at[kind, cc], set_recv.at[kind, slot], dev)

    def route_send(ring, kind, want):
        for col in range(0, WIDTH, 512):
            accs = [jnp.zeros((PAGE, 512), F32)] * 4
            for zz in range(NZ):
                page = ring[zz, :, col:col + 512].astype(F32)
                accs = [jnp.where(want(zz, cc), page, accs[cc]) for cc in range(4)]
            for cc in range(4):
                pick_out[kind, cc, :, col:col + 512] = accs[cc].astype(BF16)
        for cc in range(4):
            dev, here = route_to(kind, cc)

            @pl.when(jnp.logical_not(here))
            def _():
                route_copy(kind, cc, c, dev).start()

            @pl.when(here)
            def _():
                pick_in[kind, cc] = pick_out[kind, cc]

    def route_take(kind):
        for cc in range(4):
            @pl.when(jnp.logical_not(jnp.logical_and(c == cc, same) if not kind else c == cc))
            def _():
                route_copy(kind, cc, cc, core).wait_recv()
        return sum(pick_in[kind, cc].astype(F32) for cc in range(4)).astype(BF16)

    def route_drain(kind):
        for cc in range(4):
            dev, here = route_to(kind, cc)

            @pl.when(jnp.logical_not(here))
            def _():
                route_copy(kind, cc, c, dev).wait_send()

    def want_in(zz, cc):
        return ints[z * 4 + cc, 0:1, 0:1] == zz * 4 + c

    remote(yhi_w(0), yhi_w(0), cross_send.at[NZ], cross_recv.at[NZ], cross).wait_recv()
    z_first(2, yhi_w)
    z_step(1, own_w, 1, True)
    y_go(-1)
    y_go(1)
    two_second(0)

    @pl.when(apart)
    def _():
        for n in range(2):
            part_taken(n).wait_recv()
            hg.first(n)

    z_step(2, yhi_w, 1, False)
    z_step(1, own_w, 2, True)
    y_go(-2)
    y_go(2)
    cross_take(0)
    swap(1, 0)
    for j in (1, 2, 3):
        src = set_peer(4 - j)
        remote(ints.at[src], ints.at[src], int_send.at[j - 1], int_recv.at[j - 1], core).wait_recv()
    page_load.wait()
    two_last(0)
    route_send(pages, 0, want_in)
    z_step(2, yhi_w, 2, False)
    z_step(1, own_w, 3, True)
    y_go(-3)
    y_go(3)
    hg.second(0, True)
    hg.second(1, False)
    z_step(2, yhi_w, 3, False)
    z_step(1, own_w, 4, True)
    y_go(4)
    hid[pl.ds(pl.multiple_of((k * 4 + x) * TOK + KEEP, 16), PAGE), :] = route_take(0)
    hg.direct(2)
    for dz in (-1, 1, -2, 2):
        y_take(dz)
        swap(0, dz)
        swap(1, dz)
    hg.third(0)
    hg.third(1)
    for dz in (-3, 3):
        y_take(dz)
        swap(0, dz)
        swap(1, dz)
    z_step(2, yhi_w, 4, False)
    y_take(4)
    swap(0, 4)
    swap(1, 4)

    @pl.when(same)
    def _():
        own_loads(lambda copy: copy.wait())

    @pl.when(apart)
    def _():
        shared_copies(lambda copy: copy.wait_recv())

    ends = [info[r, 0:1, 0:1] for r in range(REQS)]

    def segment(pos, bounds):
        seg = jnp.zeros(pos.shape, jnp.int32)
        for r in range(REQS):
            seg = seg + (pos >= bounds[r]).astype(jnp.int32)
        return seg

    kid[:, 0:SEQ] = segment(lax.broadcasted_iota(jnp.int32, (8, SEQ), 1), ends)
    for r in range(REQS):
        j = lax.broadcasted_iota(jnp.int32, (8, TXT), 1)
        kid[:, SEQ + r * TXT:SEQ + (r + 1) * TXT] = jnp.where(j < info[REQS + r, 0:1, 0:1], r, -1)

    wout_load.wait()
    hg.second(2, None)
    hg.third(2)
    for item in (0, 1):
        for dz in range(NZ):
            swap_wait(item, dz)
    for n in range(2):
        hg.last(n)

    def rows_of(start, size=QB):
        return pl.ds(pl.multiple_of(start, 128), size)

    def project(blocks):
        at = [pl.ds(pl.multiple_of(first, 16), size) for first, size in blocks]
        w = jnp.concatenate([wgt[6 * k + n] for n in range(3)] + [wgt[3 + n] for n in range(3)], axis=1)
        a = jnp.concatenate([hid[rows, :] for rows in at], axis=0)
        y = jnp.dot(a, w, preferred_element_type=F32).astype(BF16)
        done = 0
        for rows, (_, size) in zip(at, blocks):
            for n, ref in enumerate((qry, keys, vals)):
                for m in range(2):
                    ref[m, rows, :] = y[done:done + size, (3 * m + n) * DIM:(3 * m + n + 1) * DIM]
            done += size

    def attend(q, pos, m):
        s = lax.dot_general(q, keys[m], (((1,), (1,)), ((), ())), preferred_element_type=F32)
        s = jnp.where(segment(pos, ends) == kid[0:1, :], s, NEG_FILL)
        best = jnp.max(s, axis=1, keepdims=True)
        w = jnp.exp2((s - best) * EXP_SCALE)
        total_w = jnp.sum(w, axis=1, keepdims=True)
        o = jnp.dot(w.astype(BF16), vals[m], preferred_element_type=F32)
        return (o / total_w).astype(BF16)

    def gated(ref, rows, start, heads, bounds, gates):
        size = heads[0].shape[0]
        seg = segment(start + lax.broadcasted_iota(jnp.int32, (size, 1), 0), bounds)
        a = jnp.concatenate(heads, axis=1)

        for n in range(3):
            cols = pl.ds(n * 512, 512)
            proj = jnp.dot(a, wout[:, cols], preferred_element_type=F32)
            scale = gates[3:4, cols]
            for r in (2, 1, 0):
                scale = jnp.where(seg == r, gates[r:r + 1, cols], scale)
            ref[rows, cols] = (ref[rows, cols].astype(F32) + scale * proj).astype(BF16)

    def item_of(n, kk, xx):
        is_b = jnp.logical_or(n == 1, n == 3)
        tok_a = jnp.where(n == 0, 0, jnp.where(n == 2, 2, jnp.where(n == 4, 1, 3)))
        tok_b = kk * 2 + jnp.where(n == 1, 0, 1)
        head = 3 * xx + jnp.where(is_b, 1, 2 * kk)
        return is_b.astype(jnp.int32), head, jnp.where(is_b, tok_b, tok_a) * QB

    def mix_at(n, kk, xx):
        _, head, tok = item_of(n, kk, xx)
        return mix.at[head, rows_of(tok), :]

    mg = Gather(mg_send, mg_recv, mix_at)

    def project_kept(t, carry):
        project([(2 * t * TOK, KEEP), ((2 * t + 1) * TOK, KEEP)])
        return carry

    lax.fori_loop(0, 4, project_kept, 0)
    hg.last(2)
    project([(d * TOK + KEEP, PAGE) for d in range(8)])

    def step_one(n, carry):
        m, head, tok = item_of(n, k, x)
        pos = tok + lax.broadcasted_iota(jnp.int32, (QB, 1), 0)
        mix[head, rows_of(tok), :] = attend(qry[m, rows_of(tok), :], pos, m)
        mg.first(n)

        @pl.when(n >= 3)
        def _():
            mg.second(n - 3, (n - 3) % 2 == 0)
        return carry

    lax.fori_loop(0, 6, step_one, 0)

    def widen(t):
        rows = rows_of(t * QB)
        gated(hid, rows, t * QB, [mix[h, rows, :] for h in range(HEADS)], ends, gate_w)
        project([(t * QB, QB)])

    for n in range(3):
        hg.drain(n)
    mg.third(0)
    mg.second(3, False)
    mg.third(1)
    mg.last(0)
    mg.last(1)
    widen(0)
    mg.second(4, True)
    mg.second(5, False)
    mg.third(2)
    mg.third(3)
    mg.last(2)
    widen(2)
    mg.third(4)
    mg.third(5)
    mg.last(3)
    mg.last(4)
    widen(1)
    mg.last(5)
    widen(3)

    home_local = pltpu.make_async_copy(hid.at[rows_of(p * TOK, TOK), :], home, home_recv)
    home_copy = remote(hid.at[rows_of(p4 * TOK, TOK), :], home, home_send, home_recv, partner)

    @pl.when(same)
    def _():
        home_local.start()

    @pl.when(apart)
    def _():
        home_copy.start()

    def send_home(src, dst, send, recv, d, sent):
        here = jnp.logical_and(same, d == p)

        if not sent:
            @pl.when(here)
            def _():
                pltpu.make_async_copy(src, dst, recv).start()

        @pl.when(jnp.logical_not(here))
        def _():
            copy = remote(src, dst, send, recv, (work_g, d))
            if sent:
                copy.wait_send()
            else:
                copy.start()

    def page_piece(n, sent):
        head = 3 * x + jnp.where(n < 8, 2 * k, 1)
        d = jnp.where(n < 8, n, k * 4 + n - 8)
        send_home(mine_page.at[n], fin_page.at[head], pa_send.at[n], pa_recv.at[head], d, sent)

    def piece(n, half, sent):
        m = (n >= 4).astype(jnp.int32)
        head = 3 * x + jnp.where(n < 4, 2 * k, 1)
        d = jnp.where(n < 4, 2 * n, k * 4 + 2 * (n - 4)) + half
        send_home(mine.at[n, half], fin.at[head], aa_send.at[n, half], aa_recv.at[head], d, sent)
        return m, d

    def block_pos(rows, block, first):
        i = lax.broadcasted_iota(jnp.int32, (rows, 1), 0)
        return first + i + (i // block) * (TOK - block)

    for m, count, first in ((0, 8, 0), (1, 4, k * 4)):
        q = jnp.concatenate(
            [qry[m, pl.ds(pl.multiple_of((first + j) * TOK + KEEP, 16), PAGE), :] for j in range(count)], axis=0)
        o = attend(q, block_pos(count * PAGE, PAGE, first * TOK + KEEP), m)
        for j in range(count):
            mine_page[8 * m + j] = o[j * PAGE:(j + 1) * PAGE]

    def send_page(n, carry):
        page_piece(n, False)
        return carry

    lax.fori_loop(0, 12, send_page, 0)

    def step_two(n, carry):
        m = (n >= 4).astype(jnp.int32)
        d = jnp.where(n < 4, 2 * n, k * 4 + 2 * (n - 4))
        q = jnp.concatenate(
            [qry[m, pl.ds(pl.multiple_of((d + j) * TOK, 128), KEEP), :] for j in range(2)], axis=0)
        o = attend(q, block_pos(2 * KEEP, KEEP, d * TOK), m)
        for half in (0, 1):
            mine[n, half] = o[half * KEEP:(half + 1) * KEEP]
        for half in (0, 1):
            piece(n, half, False)
        return carry

    def take_heads(ref, recv):
        def take(h, carry):
            remote(ref.at[h], ref.at[h], aa_send.at[0, 0], recv.at[h], core).wait_recv()
            return carry

        lax.fori_loop(0, HEADS, take, 0)

    lax.fori_loop(0, 2, step_two, 0)
    take_heads(fin_page, pa_recv)
    home_copy.wait_recv()
    gated(home, pl.ds(KEEP, PAGE), p * TOK + KEEP, [fin_page[h] for h in range(HEADS)], own_ends, gate)
    back[z, :, 0:WIDTH] = home[KEEP:TOK, :]
    back[z, :, WIDTH:] = jnp.full((PAGE, TAG), inc[0, 0], jnp.int32).astype(F32).astype(BF16)

    two_first(3)
    lax.fori_loop(2, 6, step_two, 0)
    two_second(3)
    take_heads(fin, aa_recv)
    gated(home, pl.ds(0, KEEP), p * TOK, [fin[h] for h in range(HEADS)], own_ends, gate)
    out[0:KEEP, :] = home[0:KEEP, :]
    two_last(3)

    def want_back(zz, cc):
        return back[zz, :, WIDTH:WIDTH + 1].astype(F32) == (z * 4 + cc).astype(F32)

    route_send(back, 1, want_back)
    out[KEEP:TOK, :] = route_take(1)

    for copy in pending:
        copy.wait_send()
    route_drain(0)
    route_drain(1)

    @pl.when(same)
    def _():
        shared_copies(lambda copy: copy.wait_send())

    @pl.when(apart)
    def _():
        home_copy.wait_send()
        for n in range(2):
            part_copy(n).wait_send()

    def drain(n, carry):
        mg.drain(n)
        for half in (0, 1):
            piece(n, half, True)
            page_piece(2 * n + half, True)
        return carry

    lax.fori_loop(0, 6, drain, 0)


def pinned(array):
    return pltpu.with_memory_space_constraint(array, pltpu.HBM)


def shards(latent, incoming, req_pages, text_len, gate_scale, text_keys, text_values, w_query, w_key, w_value, w_out):
    vm = pl.BlockSpec(memory_space=pltpu.VMEM)
    hb = pl.BlockSpec(memory_space=pltpu.HBM)
    dma = pltpu.SemaphoreType.DMA
    return pl.pallas_call(
        kernel,
        out_shape=jax.ShapeDtypeStruct((TOK, WIDTH), BF16),
        in_specs=[hb] * 11,
        out_specs=vm,
        scratch_shapes=[
            pltpu.VMEM((SEQ, WIDTH), BF16),
            pltpu.VMEM((TOK, WIDTH), BF16),
            pltpu.VMEM((BLOCKS, WIDTH, DIM), BF16),
            pltpu.VMEM((WIDTH, WIDTH), BF16),
            pltpu.VMEM((HEADS, SEQ, DIM), BF16),
            pltpu.VMEM((2, KEYS, DIM), BF16),
            pltpu.VMEM((2, KEYS, DIM), BF16),
            pltpu.VMEM((2, SEQ, DIM), BF16),
            pltpu.VMEM((6, 2, KEEP, DIM), BF16),
            pltpu.VMEM((HEADS, KEEP, DIM), BF16),
            pltpu.VMEM((12, PAGE, DIM), BF16),
            pltpu.VMEM((HEADS, PAGE, DIM), BF16),
            pltpu.VMEM((8, KEYS), jnp.int32),
            pltpu.VMEM((NZ, PAGE, WIDTH), BF16),
            pltpu.VMEM((NZ, PAGE, WIDTH + TAG), BF16),
            pltpu.VMEM((32, 8, 128), jnp.int32),
            pltpu.VMEM((2, 4, PAGE, WIDTH), BF16),
            pltpu.VMEM((2, 4, PAGE, WIDTH), BF16),
            pltpu.VMEM((2 * REQS, 8, 128), jnp.int32),
            pltpu.VMEM((REQS, WIDTH), F32),
            pltpu.SMEM((1, 1), jnp.int32),
            pltpu.SMEM((1, REQS), jnp.int32),
            pltpu.SMEM((1, REQS), jnp.int32),
            pltpu.VMEM((REQS, WIDTH), F32),
            dma((12,)), dma((BLOCKS,)),
            dma((4, 8)), dma((4, 8)),
            dma((2, NZ)), dma((2, NZ)),
            dma((NZ + 1,)), dma((NZ + 1,)),
            dma((NZ,)), dma((NZ,)),
            dma((3,)), dma((3,)),
            dma((2, 4)), dma((2, 4)),
            dma((2,)), dma((2,)),
            dma((6,)), dma((6,)),
            dma((3, 7)), dma((3, 7)),
            dma((6, 7)), dma((6, 7)),
            dma, dma,
            dma((6, 2)), dma((HEADS,)),
            dma((12,)), dma((HEADS,)),
        ],
        compiler_params=pltpu.CompilerParams(
            collective_id=0, has_side_effects=True, vmem_limit_bytes=50 * 1024 * 1024),
        cost_estimate=pl.CostEstimate(flops=14_000_000_000, bytes_accessed=10_000_000, transcendentals=5_000_000),
    )(
        pinned(latent),
        incoming,
        pinned(req_pages),
        pinned(text_len),
        pinned(gate_scale[0]),
        pinned(text_keys.reshape(REQS * TXT, WIDTH)),
        pinned(text_values.reshape(REQS * TXT, WIDTH)),
        pinned(w_query),
        pinned(w_key),
        pinned(w_value),
        pinned(w_out),
    )


def solution(mesh):
    in_specs = (
        P(("grp", "patch"), None),
        P("patch", "grp"),
        P("grp", None),
        P("grp", None),
        P("grp", None, None),
        P("grp", None, None, None),
        P("grp", None, None, None),
        P("grp", None),
        P("grp", None),
        P("grp", None),
        P(),
    )
    return jax.shard_map(
        shards, mesh=mesh, in_specs=in_specs, out_specs=P(("grp", "patch"), None), check_vma=False)
```

```python
import math

import jax
import jax.numpy as jnp
from jax import lax
from jax.experimental import pallas as pl
from jax.experimental.pallas import tpu as pltpu
from jax.sharding import PartitionSpec as P

MESH = pl.DeviceIdType.MESH
HEADS = 12
DIM = 128
WIDTH = 1536
PAGE = 16
REQS = 4
TXT = 128
TOK = 128
SEQ = 1024
KEEP = TOK - PAGE
NZ = 8
WROWS = 48
BLOCKS = 10
KEYS = SEQ + REQS * TXT
QB = 256
NEG_FILL = -1e30
TAG = 128
F32 = jnp.float32
BF16 = jnp.bfloat16
EXP_SCALE = math.log2(math.e) / math.sqrt(DIM)

PARTS = ((0, 64), (64, 48), (112, 16))


def kernel(
    lat, inc_h, req_pages_h, text_len_h, gate_h, text_k, text_v, w_q, w_k, w_v, w_o, out,
    hid, home, wgt, wout, mix, keys, vals, qry, mine, fin, mine_page, fin_page, kid,
    pages, back, ints, pick_out, pick_in, info, gate_w,
    inc, req_pages, text_len, gate, local_sem, weight_sem, z_send, z_recv, swap_send, swap_recv, cross_send, cross_recv, pair_send, pair_recv,
    int_send, int_recv, set_send, set_recv, part_send, part_recv, text_send, text_recv,
    hg_send, hg_recv, mg_send, mg_recv, home_send, home_recv, aa_send, aa_recv, pa_send, pa_recv,
):
    g = lax.axis_index("grp")
    p = lax.axis_index("patch")
    z, c = g // 4, g % 4
    yh, k = c // 2, c % 2
    x, yl = p % 4, p // 4
    same = k == yl
    apart = k != yl
    p4 = (p + 4) % 8
    core_g = g + 1 - 2 * k
    work_g = z * 4 + yh * 2 + yl

    right, left, far = (g, yl * 4 + (x + 1) % 4), (g, yl * 4 + (x + 3) % 4), (g, yl * 4 + (x + 2) % 4)
    up, down = ((g + 4) % 32, p), ((g + 28) % 32, p)
    up2, down2 = ((g + 8) % 32, p), ((g + 24) % 32, p)
    yhi_g = z * 4 + (c + 2) % 4
    core, partner = (core_g, p), (core_g, p4)
    pair, cross = (g, p4), (yhi_g, p4)
    mine_first, other_first = 5 * yl, 5 - 5 * yl

    def set_peer(j):
        return z * 4 + (c + j) % 4

    def zdev(dz, cc):
        return ((z + dz) % NZ) * 4 + cc

    head_a, head_b = 3 * x + 2 * k, 3 * x + 1

    def cols_of(head):
        return pl.ds(pl.multiple_of(head * DIM, DIM), DIM)

    def wrows(gg, first=0, count=BLOCKS):
        return wgt.at[pl.ds(first, count), pl.ds(pl.multiple_of(gg * WROWS, 16), WROWS), :]

    my_rows = pl.ds(pl.multiple_of(g * WROWS, 16), WROWS)
    loads = []
    for b in range(BLOCKS):
        w = (w_q, w_k, w_v)[b % 3]
        loads.append(pltpu.make_async_copy(w.at[:, cols_of(3 * x + b // 3 % 3)], wgt.at[b, my_rows, :], weight_sem.at[b]))
    my_hid = pl.ds(pl.multiple_of(p * TOK, TOK), KEEP)

    def text_copies(fn, heads):
        for n, (src, dst) in enumerate(((text_k, keys), (text_v, vals))):
            for m in range(2):
                fn(src.at[:, cols_of(heads[m])], dst.at[m, pl.ds(SEQ, REQS * TXT), :], 2 * n + m)

    def own_loads(fn):
        text_copies(lambda src, dst, n: fn(pltpu.make_async_copy(src, dst, local_sem.at[n])), (head_a, head_b))
        fn(pltpu.make_async_copy(lat.at[pl.ds(0, KEEP), :], hid.at[my_hid, :], local_sem.at[4]))
        fn(pltpu.make_async_copy(gate_h, gate_w, local_sem.at[5]))

    wout_load = pltpu.make_async_copy(w_o, wout, local_sem.at[6])
    page_load = pltpu.make_async_copy(lat.at[pl.ds(KEEP, PAGE), :], pages.at[z], local_sem.at[7])
    small_loads = [
        pltpu.make_async_copy(src, dst, local_sem.at[8 + n])
        for n, (src, dst) in enumerate(((inc_h, inc), (req_pages_h, req_pages), (text_len_h, text_len), (gate_h, gate)))]
    page_load.start()
    for load in small_loads + loads:
        load.start()

    barrier = pltpu.get_barrier_semaphore()
    greeted = [up, down, up2, down2]
    plane = z * 4 + yh * 2
    for dk in range(2):
        for dp in range(8):
            if (dk, dp) != (0, 0):
                greeted.append((plane + (k + dk) % 2, (p + dp) % 8))
    other_plane = z * 4 + (1 - yh) * 2
    greeted += [(other_plane + dk, pp) for dk in range(2) for pp in (p, p4)]
    for peer in greeted:
        pl.semaphore_signal(barrier, inc=1, device_id=peer, device_id_type=MESH)
    pl.semaphore_wait(barrier, len(greeted))

    pending = []

    def remote(src, dst, send, recv, dev):
        return pltpu.make_async_remote_copy(
            src_ref=src, dst_ref=dst, send_sem=send, recv_sem=recv, device_id=dev, device_id_type=MESH)

    def go(*args):
        copy = remote(*args)
        copy.start()
        pending.append(copy)

    Z_FROM = (-1, -2, -3, 1, 2, 3, 4)

    def z_copy(item, at, slot, dz, dev):
        return remote(at(dz), at(dz), z_send.at[item, slot], z_recv.at[item, slot], dev)

    def z_go(item, at, slot, dz, dev):
        copy = z_copy(item, at, slot, dz, dev)
        copy.start()
        pending.append(copy)

    def z_wait(item, at, slot):
        z_copy(item, at, slot, Z_FROM[slot], up).wait_recv()

    def z_first(item, at):
        z_go(item, at, 0, 0, up)
        z_go(item, at, 3, 0, down)

    def z_step(item, at, step, last_up):
        if step == 4:
            z_wait(item, at, 6)
            return
        z_wait(item, at, step - 1)
        if step < 3:
            z_go(item, at, step, -step, up)
        elif last_up:
            z_go(item, at, 6, -3, up)
        z_wait(item, at, 2 + step)
        if step < 3:
            z_go(item, at, 3 + step, step, down)
        elif not last_up:
            z_go(item, at, 6, 3, down)

    def two_copy(item, slot, dz, dev, src=None):
        ring, first, count = pages if item == 0 else back, 0, WIDTH + (TAG if item else 0)
        if slot == 6:
            count = WIDTH // 2
        if slot == 7:
            first, count = WIDTH // 2, count - WIDTH // 2
        ref = ring.at[(z + dz) % NZ, :, pl.ds(first, count)]
        return remote(ref if src is None else src, ref, z_send.at[item, slot], z_recv.at[item, slot], dev)

    def two_go(item, slot, dz, dev, src=None):
        copy = two_copy(item, slot, dz, dev, src)
        copy.start()
        pending.append(copy)

    def two_first(item, src=None):
        two_go(item, 1, 0, up2, src)
        two_go(item, 4, 0, down2, src)
        two_go(item, 0, 0, up, src)
        two_go(item, 3, 0, down, src)

    def two_second(item):
        two_copy(item, 1, -2, up).wait_recv()
        two_go(item, 6, -2, up2)
        two_go(item, 2, -2, up)
        two_copy(item, 4, 2, up).wait_recv()
        two_go(item, 7, 2, down2)
        two_go(item, 5, 2, down)

    def two_last(item):
        for slot, dz in ((0, -1), (3, 1), (2, -3), (5, 3), (6, 4), (7, 4)):
            two_copy(item, slot, dz, up).wait_recv()

    def own_w(dz):
        return wrows(zdev(dz, c), mine_first, 5)

    def yhi_w(dz):
        return wrows(zdev(dz, (c + 2) % 4), mine_first, 5)

    def y_go(dz):
        go(own_w(dz), own_w(dz), pair_send.at[dz % NZ], pair_recv.at[dz % NZ], pair)
        go(own_w(dz), own_w(dz), cross_send.at[dz % NZ], cross_recv.at[dz % NZ], cross)

    def y_take(dz):
        ref = wrows(zdev(dz, c), other_first, 5)
        remote(ref, ref, pair_send.at[dz % NZ], pair_recv.at[dz % NZ], pair).wait_recv()
        cross_take(dz)

    def cross_take(dz):
        ref = wrows(zdev(dz, (c + 2) % 4), other_first, 5)
        remote(ref, ref, cross_send.at[dz % NZ], cross_recv.at[dz % NZ], cross).wait_recv()

    def swap(item, dz):
        ref = wrows(zdev(dz, (c + 2 * item) % 4))
        go(ref, ref, swap_send.at[item, dz % NZ], swap_recv.at[item, dz % NZ], core)

    def swap_wait(item, dz):
        ref = wrows(zdev(dz, (2 * yh + 1 - k + 2 * item) % 4))
        remote(ref, ref, swap_send.at[item, dz % NZ], swap_recv.at[item, dz % NZ], core).wait_recv()

    X_FROM = (3, 1, 2, 0, 3, 1, 2)

    class Gather:
        def __init__(self, send, recv, at):
            self.send, self.recv, self.at = send, recv, at

        def copy(self, n, slot, kk, dx, dev, src=None):
            ref = self.at(n, kk, (x + dx) % 4)
            return remote(ref if src is None else src, ref, self.send.at[n, slot], self.recv.at[n, slot], dev)

        def go(self, n, slot, dx, dev, src=None):
            self.copy(n, slot, k, dx, dev, src).start()

        def first(self, n, src=None):
            self.go(n, 0, 0, right, src)
            self.go(n, 1, 0, left, src)
            self.go(n, 3, 0, core, src)

        def direct(self, n):
            self.first(n)
            self.go(n, 2, 0, far)

        def wait(self, n, slot):
            self.copy(n, slot, k if slot < 3 else 1 - k, X_FROM[slot], core).wait_recv()

        def second(self, n, far_right):
            self.wait(n, 0)
            if far_right is True:
                self.go(n, 2, 3, right)
            self.go(n, 4, 3, core)
            self.wait(n, 1)
            if far_right is False:
                self.go(n, 2, 1, left)
            if far_right is not None and not isinstance(far_right, bool):
                @pl.when(far_right)
                def _():
                    self.go(n, 2, 3, right)

                @pl.when(jnp.logical_not(far_right))
                def _():
                    self.go(n, 2, 1, left)
            self.go(n, 5, 1, core)

        def third(self, n):
            self.wait(n, 2)
            self.go(n, 6, 2, core)

        def last(self, n):
            for slot in (3, 4, 5, 6):
                self.wait(n, slot)

        def drain(self, n):
            for slot in range(7):
                self.copy(n, slot, k, 0, core).wait_send()

    def hid_at(n, kk, xx):
        first, rows = PARTS[n]
        return hid.at[pl.ds(pl.multiple_of((kk * 4 + xx) * TOK + first, 16), rows), :]

    hg = Gather(hg_send, hg_recv, hid_at)

    def lat_part(n):
        return lat.at[pl.ds(*PARTS[n]), :]

    def part_copy(n):
        first, rows = PARTS[n]
        dst = hid.at[pl.ds(pl.multiple_of(p * TOK + first, 16), rows), :]
        return remote(lat_part(n), dst, part_send.at[n], part_recv.at[n], partner)

    def part_taken(n):
        return remote(lat_part(n), hid_at(n, k, x), part_send.at[n], part_recv.at[n], partner)

    for load in loads:
        load.wait()
    z_first(1, own_w)
    other_half = wrows(g, other_first, 5)
    go(other_half, other_half, cross_send.at[NZ], cross_recv.at[NZ], cross)
    go(own_w(0), own_w(0), cross_send.at[0], cross_recv.at[0], cross)
    two_first(0, lat.at[pl.ds(KEEP, PAGE), :])

    @pl.when(same)
    def _():
        for n in range(2):
            hg.first(n, lat_part(n))

    @pl.when(apart)
    def _():
        for n in range(2):
            part_copy(n).start()

    for load in small_loads:
        load.wait()
    ints[g] = jnp.full((8, 128), inc[0, 0], jnp.int32)
    for j in (1, 2, 3):
        go(ints.at[g], ints.at[g], int_send.at[j - 1], int_recv.at[j - 1], (set_peer(j), p))
    swap(0, 0)

    own_ends = []
    total = jnp.int32(0)
    for r in range(REQS):
        total = total + req_pages[0, r] * PAGE
        own_ends.append(total)

    def shared_copies(fn):
        fn(remote(info, info, text_send.at[4], text_recv.at[4], core))
        fn(remote(gate_h, gate_w, text_send.at[5], text_recv.at[5], core))
        text_copies(lambda src, dst, n: fn(remote(src, dst, text_send.at[n], text_recv.at[n], core)),
                    (3 * x + 2 - 2 * k, head_b))

    @pl.when(same)
    def _():
        for r in range(REQS):
            info[r] = jnp.full((8, 128), own_ends[r], jnp.int32)
            info[REQS + r] = jnp.full((8, 128), text_len[0, r], jnp.int32)
        own_loads(lambda copy: copy.start())
        shared_copies(lambda copy: copy.start())

    wout_load.start()

    def route_to(kind, cc):
        if kind:
            return (z * 4 + cc, p), c == cc
        here = yl == cc % 2
        return (z * 4 + jnp.where(here, cc, cc + 1 - 2 * (cc % 2)), jnp.where(here, p, p4)), jnp.logical_and(c == cc, same)

    def route_copy(kind, cc, slot, dev):
        return remote(pick_out.at[kind, cc], pick_in.at[kind, slot], set_send.at[kind, cc], set_recv.at[kind, slot], dev)

    def route_send(ring, kind, want):
        for col in range(0, WIDTH, 512):
            accs = [jnp.zeros((PAGE, 512), F32)] * 4
            for zz in range(NZ):
                page = ring[zz, :, col:col + 512].astype(F32)
                accs = [jnp.where(want(zz, cc), page, accs[cc]) for cc in range(4)]
            for cc in range(4):
                pick_out[kind, cc, :, col:col + 512] = accs[cc].astype(BF16)
        for cc in range(4):
            dev, here = route_to(kind, cc)

            @pl.when(jnp.logical_not(here))
            def _():
                route_copy(kind, cc, c, dev).start()

            @pl.when(here)
            def _():
                pick_in[kind, cc] = pick_out[kind, cc]

    def route_take(kind):
        for cc in range(4):
            @pl.when(jnp.logical_not(jnp.logical_and(c == cc, same) if not kind else c == cc))
            def _():
                route_copy(kind, cc, cc, core).wait_recv()
        return sum(pick_in[kind, cc].astype(F32) for cc in range(4)).astype(BF16)

    def route_drain(kind):
        for cc in range(4):
            dev, here = route_to(kind, cc)

            @pl.when(jnp.logical_not(here))
            def _():
                route_copy(kind, cc, c, dev).wait_send()

    def want_in(zz, cc):
        return ints[z * 4 + cc, 0:1, 0:1] == zz * 4 + c

    remote(yhi_w(0), yhi_w(0), cross_send.at[NZ], cross_recv.at[NZ], cross).wait_recv()
    z_first(2, yhi_w)
    z_step(1, own_w, 1, True)
    y_go(-1)
    y_go(1)
    two_second(0)

    @pl.when(apart)
    def _():
        for n in range(2):
            part_taken(n).wait_recv()
            hg.first(n)

    z_step(2, yhi_w, 1, False)
    z_step(1, own_w, 2, True)
    y_go(-2)
    y_go(2)
    cross_take(0)
    swap(1, 0)
    for j in (1, 2, 3):
        src = set_peer(4 - j)
        remote(ints.at[src], ints.at[src], int_send.at[j - 1], int_recv.at[j - 1], core).wait_recv()
    page_load.wait()
    two_last(0)
    route_send(pages, 0, want_in)
    z_step(2, yhi_w, 2, False)
    z_step(1, own_w, 3, True)
    y_go(-3)
    y_go(3)
    hg.second(0, True)
    hg.second(1, False)
    z_step(2, yhi_w, 3, False)
    z_step(1, own_w, 4, True)
    y_go(4)
    hid[pl.ds(pl.multiple_of((k * 4 + x) * TOK + KEEP, 16), PAGE), :] = route_take(0)
    hg.direct(2)
    for dz in (-1, 1, -2, 2):
        y_take(dz)
        swap(0, dz)
        swap(1, dz)
    hg.third(0)
    hg.third(1)
    for dz in (-3, 3):
        y_take(dz)
        swap(0, dz)
        swap(1, dz)
    z_step(2, yhi_w, 4, False)
    y_take(4)
    swap(0, 4)
    swap(1, 4)

    @pl.when(same)
    def _():
        own_loads(lambda copy: copy.wait())

    @pl.when(apart)
    def _():
        shared_copies(lambda copy: copy.wait_recv())

    ends = [info[r, 0:1, 0:1] for r in range(REQS)]

    def segment(pos, bounds):
        seg = jnp.zeros(pos.shape, jnp.int32)
        for r in range(REQS):
            seg = seg + (pos >= bounds[r]).astype(jnp.int32)
        return seg

    kid[:, 0:SEQ] = segment(lax.broadcasted_iota(jnp.int32, (8, SEQ), 1), ends)
    for r in range(REQS):
        j = lax.broadcasted_iota(jnp.int32, (8, TXT), 1)
        kid[:, SEQ + r * TXT:SEQ + (r + 1) * TXT] = jnp.where(j < info[REQS + r, 0:1, 0:1], r, -1)

    wout_load.wait()
    hg.second(2, None)
    hg.third(2)
    for item in (0, 1):
        for dz in range(NZ):
            swap_wait(item, dz)
    for n in range(2):
        hg.last(n)

    def rows_of(start, size=QB):
        return pl.ds(pl.multiple_of(start, 128), size)

    def project(blocks):
        at = [pl.ds(pl.multiple_of(first, 16), size) for first, size in blocks]
        w = jnp.concatenate([wgt[6 * k + n] for n in range(3)] + [wgt[3 + n] for n in range(3)], axis=1)
        a = jnp.concatenate([hid[rows, :] for rows in at], axis=0)
        y = jnp.dot(a, w, preferred_element_type=F32).astype(BF16)
        done = 0
        for rows, (_, size) in zip(at, blocks):
            for n, ref in enumerate((qry, keys, vals)):
                for m in range(2):
                    ref[m, rows, :] = y[done:done + size, (3 * m + n) * DIM:(3 * m + n + 1) * DIM]
            done += size

    def attend(q, pos, m):
        s = lax.dot_general(q, keys[m], (((1,), (1,)), ((), ())), preferred_element_type=F32)
        s = jnp.where(segment(pos, ends) == kid[0:1, :], s, NEG_FILL)
        best = jnp.max(s, axis=1, keepdims=True)
        w = jnp.exp2((s - best) * EXP_SCALE)
        total_w = jnp.sum(w, axis=1, keepdims=True)
        o = jnp.dot(w.astype(BF16), vals[m], preferred_element_type=F32)
        return (o / total_w).astype(BF16)

    def gated(ref, rows, start, heads, bounds, gates):
        size = heads[0].shape[0]
        seg = segment(start + lax.broadcasted_iota(jnp.int32, (size, 1), 0), bounds)
        a = jnp.concatenate(heads, axis=1)

        for n in range(3):
            cols = pl.ds(n * 512, 512)
            proj = jnp.dot(a, wout[:, cols], preferred_element_type=F32)
            scale = gates[3:4, cols]
            for r in (2, 1, 0):
                scale = jnp.where(seg == r, gates[r:r + 1, cols], scale)
            ref[rows, cols] = (ref[rows, cols].astype(F32) + scale * proj).astype(BF16)

    def item_of(n, kk, xx):
        is_b = jnp.logical_or(n == 1, n == 3)
        tok_a = jnp.where(n == 0, 0, jnp.where(n == 2, 2, jnp.where(n == 4, 1, 3)))
        tok_b = kk * 2 + jnp.where(n == 1, 0, 1)
        head = 3 * xx + jnp.where(is_b, 1, 2 * kk)
        return is_b.astype(jnp.int32), head, jnp.where(is_b, tok_b, tok_a) * QB

    def mix_at(n, kk, xx):
        _, head, tok = item_of(n, kk, xx)
        return mix.at[head, rows_of(tok), :]

    mg = Gather(mg_send, mg_recv, mix_at)

    def project_kept(t, carry):
        project([(2 * t * TOK, KEEP), ((2 * t + 1) * TOK, KEEP)])
        return carry

    lax.fori_loop(0, 4, project_kept, 0)
    hg.last(2)
    project([(d * TOK + KEEP, PAGE) for d in range(8)])

    def step_one(n, carry):
        m, head, tok = item_of(n, k, x)
        pos = tok + lax.broadcasted_iota(jnp.int32, (QB, 1), 0)
        mix[head, rows_of(tok), :] = attend(qry[m, rows_of(tok), :], pos, m)
        mg.first(n)

        @pl.when(n >= 2)
        def _():
            mg.second(n - 2, (n - 2) % 2 == 0)
        return carry

    lax.fori_loop(0, 6, step_one, 0)

    def widen(t):
        rows = rows_of(t * QB)
        gated(hid, rows, t * QB, [mix[h, rows, :] for h in range(HEADS)], ends, gate_w)
        project([(t * QB, QB)])

    for n in range(3):
        hg.drain(n)
    mg.third(0)
    mg.third(1)
    mg.last(0)
    mg.last(1)
    mg.second(4, True)
    widen(0)
    mg.second(5, False)
    mg.third(2)
    mg.third(3)
    mg.last(2)
    widen(2)
    mg.third(4)
    mg.third(5)
    mg.last(3)
    mg.last(4)
    widen(1)
    mg.last(5)
    widen(3)

    home_local = pltpu.make_async_copy(hid.at[rows_of(p * TOK, TOK), :], home, home_recv)
    home_copy = remote(hid.at[rows_of(p4 * TOK, TOK), :], home, home_send, home_recv, partner)

    @pl.when(same)
    def _():
        home_local.start()

    @pl.when(apart)
    def _():
        home_copy.start()

    def send_home(src, dst, send, recv, d, sent):
        here = jnp.logical_and(same, d == p)

        if not sent:
            @pl.when(here)
            def _():
                pltpu.make_async_copy(src, dst, recv).start()

        @pl.when(jnp.logical_not(here))
        def _():
            copy = remote(src, dst, send, recv, (work_g, d))
            if sent:
                copy.wait_send()
            else:
                copy.start()

    def page_piece(n, sent):
        head = 3 * x + jnp.where(n < 8, 2 * k, 1)
        d = jnp.where(n < 8, n, k * 4 + n - 8)
        send_home(mine_page.at[n], fin_page.at[head], pa_send.at[n], pa_recv.at[head], d, sent)

    def piece(n, half, sent):
        m = (n >= 4).astype(jnp.int32)
        head = 3 * x + jnp.where(n < 4, 2 * k, 1)
        d = jnp.where(n < 4, 2 * n, k * 4 + 2 * (n - 4)) + half
        send_home(mine.at[n, half], fin.at[head], aa_send.at[n, half], aa_recv.at[head], d, sent)
        return m, d

    def block_pos(rows, block, first):
        i = lax.broadcasted_iota(jnp.int32, (rows, 1), 0)
        return first + i + (i // block) * (TOK - block)

    for m, count, first in ((0, 8, 0), (1, 4, k * 4)):
        q = jnp.concatenate(
            [qry[m, pl.ds(pl.multiple_of((first + j) * TOK + KEEP, 16), PAGE), :] for j in range(count)], axis=0)
        o = attend(q, block_pos(count * PAGE, PAGE, first * TOK + KEEP), m)
        for j in range(count):
            mine_page[8 * m + j] = o[j * PAGE:(j + 1) * PAGE]

    def send_page(n, carry):
        page_piece(n, False)
        return carry

    lax.fori_loop(0, 12, send_page, 0)

    def step_two(n, carry):
        m = (n >= 4).astype(jnp.int32)
        d = jnp.where(n < 4, 2 * n, k * 4 + 2 * (n - 4))
        q = jnp.concatenate(
            [qry[m, pl.ds(pl.multiple_of((d + j) * TOK, 128), KEEP), :] for j in range(2)], axis=0)
        o = attend(q, block_pos(2 * KEEP, KEEP, d * TOK), m)
        for half in (0, 1):
            mine[n, half] = o[half * KEEP:(half + 1) * KEEP]
        for half in (0, 1):
            piece(n, half, False)
        return carry

    def take_heads(ref, recv):
        def take(h, carry):
            remote(ref.at[h], ref.at[h], aa_send.at[0, 0], recv.at[h], core).wait_recv()
            return carry

        lax.fori_loop(0, HEADS, take, 0)

    lax.fori_loop(0, 2, step_two, 0)
    take_heads(fin_page, pa_recv)
    home_copy.wait_recv()
    gated(home, pl.ds(KEEP, PAGE), p * TOK + KEEP, [fin_page[h] for h in range(HEADS)], own_ends, gate)
    back[z, :, 0:WIDTH] = home[KEEP:TOK, :]
    back[z, :, WIDTH:] = jnp.full((PAGE, TAG), inc[0, 0], jnp.int32).astype(F32).astype(BF16)

    two_first(3)
    lax.fori_loop(2, 6, step_two, 0)
    two_second(3)
    take_heads(fin, aa_recv)
    gated(home, pl.ds(0, KEEP), p * TOK, [fin[h] for h in range(HEADS)], own_ends, gate)
    out[0:KEEP, :] = home[0:KEEP, :]
    two_last(3)

    def want_back(zz, cc):
        return back[zz, :, WIDTH:WIDTH + 1].astype(F32) == (z * 4 + cc).astype(F32)

    route_send(back, 1, want_back)
    out[KEEP:TOK, :] = route_take(1)

    for copy in pending:
        copy.wait_send()
    route_drain(0)
    route_drain(1)

    @pl.when(same)
    def _():
        shared_copies(lambda copy: copy.wait_send())

    @pl.when(apart)
    def _():
        home_copy.wait_send()
        for n in range(2):
            part_copy(n).wait_send()

    def drain(n, carry):
        mg.drain(n)
        for half in (0, 1):
            piece(n, half, True)
            page_piece(2 * n + half, True)
        return carry

    lax.fori_loop(0, 6, drain, 0)


def pinned(array):
    return pltpu.with_memory_space_constraint(array, pltpu.HBM)


def shards(latent, incoming, req_pages, text_len, gate_scale, text_keys, text_values, w_query, w_key, w_value, w_out):
    vm = pl.BlockSpec(memory_space=pltpu.VMEM)
    hb = pl.BlockSpec(memory_space=pltpu.HBM)
    dma = pltpu.SemaphoreType.DMA
    return pl.pallas_call(
        kernel,
        out_shape=jax.ShapeDtypeStruct((TOK, WIDTH), BF16),
        in_specs=[hb] * 11,
        out_specs=vm,
        scratch_shapes=[
            pltpu.VMEM((SEQ, WIDTH), BF16),
            pltpu.VMEM((TOK, WIDTH), BF16),
            pltpu.VMEM((BLOCKS, WIDTH, DIM), BF16),
            pltpu.VMEM((WIDTH, WIDTH), BF16),
            pltpu.VMEM((HEADS, SEQ, DIM), BF16),
            pltpu.VMEM((2, KEYS, DIM), BF16),
            pltpu.VMEM((2, KEYS, DIM), BF16),
            pltpu.VMEM((2, SEQ, DIM), BF16),
            pltpu.VMEM((6, 2, KEEP, DIM), BF16),
            pltpu.VMEM((HEADS, KEEP, DIM), BF16),
            pltpu.VMEM((12, PAGE, DIM), BF16),
            pltpu.VMEM((HEADS, PAGE, DIM), BF16),
            pltpu.VMEM((8, KEYS), jnp.int32),
            pltpu.VMEM((NZ, PAGE, WIDTH), BF16),
            pltpu.VMEM((NZ, PAGE, WIDTH + TAG), BF16),
            pltpu.VMEM((32, 8, 128), jnp.int32),
            pltpu.VMEM((2, 4, PAGE, WIDTH), BF16),
            pltpu.VMEM((2, 4, PAGE, WIDTH), BF16),
            pltpu.VMEM((2 * REQS, 8, 128), jnp.int32),
            pltpu.VMEM((REQS, WIDTH), F32),
            pltpu.SMEM((1, 1), jnp.int32),
            pltpu.SMEM((1, REQS), jnp.int32),
            pltpu.SMEM((1, REQS), jnp.int32),
            pltpu.VMEM((REQS, WIDTH), F32),
            dma((12,)), dma((BLOCKS,)),
            dma((4, 8)), dma((4, 8)),
            dma((2, NZ)), dma((2, NZ)),
            dma((NZ + 1,)), dma((NZ + 1,)),
            dma((NZ,)), dma((NZ,)),
            dma((3,)), dma((3,)),
            dma((2, 4)), dma((2, 4)),
            dma((2,)), dma((2,)),
            dma((6,)), dma((6,)),
            dma((3, 7)), dma((3, 7)),
            dma((6, 7)), dma((6, 7)),
            dma, dma,
            dma((6, 2)), dma((HEADS,)),
            dma((12,)), dma((HEADS,)),
        ],
        compiler_params=pltpu.CompilerParams(
            collective_id=0, has_side_effects=True, vmem_limit_bytes=50 * 1024 * 1024),
        cost_estimate=pl.CostEstimate(flops=14_000_000_000, bytes_accessed=10_000_000, transcendentals=5_000_000),
    )(
        pinned(latent),
        incoming,
        pinned(req_pages),
        pinned(text_len),
        pinned(gate_scale[0]),
        pinned(text_keys.reshape(REQS * TXT, WIDTH)),
        pinned(text_values.reshape(REQS * TXT, WIDTH)),
        pinned(w_query),
        pinned(w_key),
        pinned(w_value),
        pinned(w_out),
    )


def solution(mesh):
    in_specs = (
        P(("grp", "patch"), None),
        P("patch", "grp"),
        P("grp", None),
        P("grp", None),
        P("grp", None, None),
        P("grp", None, None, None),
        P("grp", None, None, None),
        P("grp", None),
        P("grp", None),
        P("grp", None),
        P(),
    )
    return jax.shard_map(
        shards, mesh=mesh, in_specs=in_specs, out_specs=P(("grp", "patch"), None), check_vma=False)
```

```python
import math

import jax
import jax.numpy as jnp
from jax import lax
from jax.experimental import pallas as pl
from jax.experimental.pallas import tpu as pltpu
from jax.sharding import PartitionSpec as P

MESH = pl.DeviceIdType.MESH
HEADS = 12
DIM = 128
WIDTH = 1536
PAGE = 16
REQS = 4
TXT = 128
TOK = 128
SEQ = 1024
KEEP = TOK - PAGE
NZ = 8
WROWS = 48
BLOCKS = 10
KEYS = SEQ + REQS * TXT
QB = 256
NEG_FILL = -1e30
TAG = 128
F32 = jnp.float32
BF16 = jnp.bfloat16
EXP_SCALE = math.log2(math.e) / math.sqrt(DIM)

PARTS = ((0, 64), (64, 48), (112, 16))


def kernel(
    lat, inc_h, req_pages_h, text_len_h, gate_h, text_k, text_v, w_q, w_k, w_v, w_o, out,
    hid, home, wgt, wout, mix, keys, vals, qry, mine, fin, mine_page, fin_page, kid,
    pages, back, ints, pick_out, pick_in, info, gate_w,
    inc, req_pages, text_len, gate, local_sem, weight_sem, z_send, z_recv, swap_send, swap_recv, cross_send, cross_recv, pair_send, pair_recv,
    int_send, int_recv, set_send, set_recv, part_send, part_recv, text_send, text_recv,
    hg_send, hg_recv, mg_send, mg_recv, home_send, home_recv, aa_send, aa_recv, pa_send, pa_recv,
):
    g = lax.axis_index("grp")
    p = lax.axis_index("patch")
    z, c = g // 4, g % 4
    yh, k = c // 2, c % 2
    x, yl = p % 4, p // 4
    same = k == yl
    apart = k != yl
    p4 = (p + 4) % 8
    core_g = g + 1 - 2 * k
    work_g = z * 4 + yh * 2 + yl

    right, left, far = (g, yl * 4 + (x + 1) % 4), (g, yl * 4 + (x + 3) % 4), (g, yl * 4 + (x + 2) % 4)
    up, down = ((g + 4) % 32, p), ((g + 28) % 32, p)
    up2, down2 = ((g + 8) % 32, p), ((g + 24) % 32, p)
    yhi_g = z * 4 + (c + 2) % 4
    core, partner = (core_g, p), (core_g, p4)
    pair, cross = (g, p4), (yhi_g, p4)
    mine_first, other_first = 5 * yl, 5 - 5 * yl

    def set_peer(j):
        return z * 4 + (c + j) % 4

    def zdev(dz, cc):
        return ((z + dz) % NZ) * 4 + cc

    head_a, head_b = 3 * x + 2 * k, 3 * x + 1

    def cols_of(head):
        return pl.ds(pl.multiple_of(head * DIM, DIM), DIM)

    def wrows(gg, first=0, count=BLOCKS):
        return wgt.at[pl.ds(first, count), pl.ds(pl.multiple_of(gg * WROWS, 16), WROWS), :]

    my_rows = pl.ds(pl.multiple_of(g * WROWS, 16), WROWS)
    loads = []
    for b in range(BLOCKS):
        w = (w_q, w_k, w_v)[b % 3]
        loads.append(pltpu.make_async_copy(w.at[:, cols_of(3 * x + b // 3 % 3)], wgt.at[b, my_rows, :], weight_sem.at[b]))
    my_hid = pl.ds(pl.multiple_of(p * TOK, TOK), KEEP)

    def text_copies(fn, heads):
        for n, (src, dst) in enumerate(((text_k, keys), (text_v, vals))):
            for m in range(2):
                fn(src.at[:, cols_of(heads[m])], dst.at[m, pl.ds(SEQ, REQS * TXT), :], 2 * n + m)

    def own_loads(fn):
        text_copies(lambda src, dst, n: fn(pltpu.make_async_copy(src, dst, local_sem.at[n])), (head_a, head_b))
        fn(pltpu.make_async_copy(lat.at[pl.ds(0, KEEP), :], hid.at[my_hid, :], local_sem.at[4]))
        fn(pltpu.make_async_copy(gate_h, gate_w, local_sem.at[5]))

    wout_load = pltpu.make_async_copy(w_o, wout, local_sem.at[6])
    page_load = pltpu.make_async_copy(lat.at[pl.ds(KEEP, PAGE), :], pages.at[z], local_sem.at[7])
    small_loads = [
        pltpu.make_async_copy(src, dst, local_sem.at[8 + n])
        for n, (src, dst) in enumerate(((inc_h, inc), (req_pages_h, req_pages), (text_len_h, text_len), (gate_h, gate)))]
    page_load.start()
    for load in small_loads + loads:
        load.start()

    barrier = pltpu.get_barrier_semaphore()
    greeted = [up, down, up2, down2]
    plane = z * 4 + yh * 2
    for dk in range(2):
        for dp in range(8):
            if (dk, dp) != (0, 0):
                greeted.append((plane + (k + dk) % 2, (p + dp) % 8))
    other_plane = z * 4 + (1 - yh) * 2
    greeted += [(other_plane + dk, pp) for dk in range(2) for pp in (p, p4)]
    for peer in greeted:
        pl.semaphore_signal(barrier, inc=1, device_id=peer, device_id_type=MESH)
    pl.semaphore_wait(barrier, len(greeted))

    pending = []

    def remote(src, dst, send, recv, dev):
        return pltpu.make_async_remote_copy(
            src_ref=src, dst_ref=dst, send_sem=send, recv_sem=recv, device_id=dev, device_id_type=MESH)

    def go(*args):
        copy = remote(*args)
        copy.start()
        pending.append(copy)

    Z_FROM = (-1, -2, -3, 1, 2, 3, 4)

    def z_copy(item, at, slot, dz, dev):
        return remote(at(dz), at(dz), z_send.at[item, slot], z_recv.at[item, slot], dev)

    def z_go(item, at, slot, dz, dev):
        copy = z_copy(item, at, slot, dz, dev)
        copy.start()
        pending.append(copy)

    def z_wait(item, at, slot):
        z_copy(item, at, slot, Z_FROM[slot], up).wait_recv()

    def z_first(item, at):
        z_go(item, at, 0, 0, up)
        z_go(item, at, 3, 0, down)

    def z_step(item, at, step, last_up):
        if step == 4:
            z_wait(item, at, 6)
            return
        z_wait(item, at, step - 1)
        if step < 3:
            z_go(item, at, step, -step, up)
        elif last_up:
            z_go(item, at, 6, -3, up)
        z_wait(item, at, 2 + step)
        if step < 3:
            z_go(item, at, 3 + step, step, down)
        elif not last_up:
            z_go(item, at, 6, 3, down)

    def two_copy(item, slot, dz, dev, src=None):
        ring, first, count = pages if item == 0 else back, 0, WIDTH + (TAG if item else 0)
        if slot == 6:
            count = WIDTH // 2
        if slot == 7:
            first, count = WIDTH // 2, count - WIDTH // 2
        ref = ring.at[(z + dz) % NZ, :, pl.ds(first, count)]
        return remote(ref if src is None else src, ref, z_send.at[item, slot], z_recv.at[item, slot], dev)

    def two_go(item, slot, dz, dev, src=None):
        copy = two_copy(item, slot, dz, dev, src)
        copy.start()
        pending.append(copy)

    def two_first(item, src=None):
        two_go(item, 1, 0, up2, src)
        two_go(item, 4, 0, down2, src)

    def two_near(item, src=None):
        two_go(item, 0, 0, up, src)
        two_go(item, 3, 0, down, src)

    def two_second(item):
        two_copy(item, 1, -2, up).wait_recv()
        two_go(item, 6, -2, up2)
        two_go(item, 2, -2, up)
        two_copy(item, 4, 2, up).wait_recv()
        two_go(item, 7, 2, down2)
        two_go(item, 5, 2, down)

    def two_last(item):
        for slot, dz in ((0, -1), (3, 1), (2, -3), (5, 3), (6, 4), (7, 4)):
            two_copy(item, slot, dz, up).wait_recv()

    def own_w(dz):
        return wrows(zdev(dz, c), mine_first, 5)

    def yhi_w(dz):
        return wrows(zdev(dz, (c + 2) % 4), mine_first, 5)

    def y_go(dz):
        go(own_w(dz), own_w(dz), pair_send.at[dz % NZ], pair_recv.at[dz % NZ], pair)
        go(own_w(dz), own_w(dz), cross_send.at[dz % NZ], cross_recv.at[dz % NZ], cross)

    def y_take(dz):
        ref = wrows(zdev(dz, c), other_first, 5)
        remote(ref, ref, pair_send.at[dz % NZ], pair_recv.at[dz % NZ], pair).wait_recv()
        cross_take(dz)

    def cross_take(dz):
        ref = wrows(zdev(dz, (c + 2) % 4), other_first, 5)
        remote(ref, ref, cross_send.at[dz % NZ], cross_recv.at[dz % NZ], cross).wait_recv()

    def swap(item, dz):
        ref = wrows(zdev(dz, (c + 2 * item) % 4))
        go(ref, ref, swap_send.at[item, dz % NZ], swap_recv.at[item, dz % NZ], core)

    def swap_wait(item, dz):
        ref = wrows(zdev(dz, (2 * yh + 1 - k + 2 * item) % 4))
        remote(ref, ref, swap_send.at[item, dz % NZ], swap_recv.at[item, dz % NZ], core).wait_recv()

    X_FROM = (3, 1, 2, 0, 3, 1, 2)

    class Gather:
        def __init__(self, send, recv, at):
            self.send, self.recv, self.at = send, recv, at

        def copy(self, n, slot, kk, dx, dev, src=None):
            ref = self.at(n, kk, (x + dx) % 4)
            return remote(ref if src is None else src, ref, self.send.at[n, slot], self.recv.at[n, slot], dev)

        def go(self, n, slot, dx, dev, src=None):
            self.copy(n, slot, k, dx, dev, src).start()

        def first(self, n, src=None):
            self.go(n, 0, 0, right, src)
            self.go(n, 1, 0, left, src)
            self.go(n, 3, 0, core, src)

        def direct(self, n):
            self.first(n)
            self.go(n, 2, 0, far)

        def wait(self, n, slot):
            self.copy(n, slot, k if slot < 3 else 1 - k, X_FROM[slot], core).wait_recv()

        def second(self, n, far_right):
            self.wait(n, 0)
            if far_right is True:
                self.go(n, 2, 3, right)
            self.go(n, 4, 3, core)
            self.wait(n, 1)
            if far_right is False:
                self.go(n, 2, 1, left)
            if far_right is not None and not isinstance(far_right, bool):
                @pl.when(far_right)
                def _():
                    self.go(n, 2, 3, right)

                @pl.when(jnp.logical_not(far_right))
                def _():
                    self.go(n, 2, 1, left)
            self.go(n, 5, 1, core)

        def third(self, n):
            self.wait(n, 2)
            self.go(n, 6, 2, core)

        def last(self, n):
            for slot in (3, 4, 5, 6):
                self.wait(n, slot)

        def drain(self, n):
            for slot in range(7):
                self.copy(n, slot, k, 0, core).wait_send()

    def hid_at(n, kk, xx):
        first, rows = PARTS[n]
        return hid.at[pl.ds(pl.multiple_of((kk * 4 + xx) * TOK + first, 16), rows), :]

    hg = Gather(hg_send, hg_recv, hid_at)

    def lat_part(n):
        return lat.at[pl.ds(*PARTS[n]), :]

    def part_copy(n):
        first, rows = PARTS[n]
        dst = hid.at[pl.ds(pl.multiple_of(p * TOK + first, 16), rows), :]
        return remote(lat_part(n), dst, part_send.at[n], part_recv.at[n], partner)

    def part_taken(n):
        return remote(lat_part(n), hid_at(n, k, x), part_send.at[n], part_recv.at[n], partner)

    for load in loads:
        load.wait()
    z_first(1, own_w)
    other_half = wrows(g, other_first, 5)
    go(other_half, other_half, cross_send.at[NZ], cross_recv.at[NZ], cross)
    go(own_w(0), own_w(0), cross_send.at[0], cross_recv.at[0], cross)
    two_first(0, lat.at[pl.ds(KEEP, PAGE), :])

    @pl.when(same)
    def _():
        for n in range(2):
            hg.first(n, lat_part(n))

    @pl.when(apart)
    def _():
        for n in range(2):
            part_copy(n).start()

    for load in small_loads:
        load.wait()
    ints[g] = jnp.full((8, 128), inc[0, 0], jnp.int32)
    for j in (1, 2, 3):
        go(ints.at[g], ints.at[g], int_send.at[j - 1], int_recv.at[j - 1], (set_peer(j), p))
    swap(0, 0)

    own_ends = []
    total = jnp.int32(0)
    for r in range(REQS):
        total = total + req_pages[0, r] * PAGE
        own_ends.append(total)

    def shared_copies(fn):
        fn(remote(info, info, text_send.at[4], text_recv.at[4], core))
        fn(remote(gate_h, gate_w, text_send.at[5], text_recv.at[5], core))
        text_copies(lambda src, dst, n: fn(remote(src, dst, text_send.at[n], text_recv.at[n], core)),
                    (3 * x + 2 - 2 * k, head_b))

    @pl.when(same)
    def _():
        for r in range(REQS):
            info[r] = jnp.full((8, 128), own_ends[r], jnp.int32)
            info[REQS + r] = jnp.full((8, 128), text_len[0, r], jnp.int32)
        own_loads(lambda copy: copy.start())
        shared_copies(lambda copy: copy.start())

    wout_load.start()

    def route_to(kind, cc):
        if kind:
            return (z * 4 + cc, p), c == cc
        here = yl == cc % 2
        return (z * 4 + jnp.where(here, cc, cc + 1 - 2 * (cc % 2)), jnp.where(here, p, p4)), jnp.logical_and(c == cc, same)

    def route_copy(kind, cc, slot, dev):
        return remote(pick_out.at[kind, cc], pick_in.at[kind, slot], set_send.at[kind, cc], set_recv.at[kind, slot], dev)

    def route_send(ring, kind, want):
        for cc in range(4):
            wanted = [want(zz, cc) for zz in range(NZ)]
            for col in range(0, WIDTH, DIM):
                acc = jnp.zeros((PAGE, DIM), F32)
                for zz in range(NZ):
                    acc = jnp.where(wanted[zz], ring[zz, :, col:col + DIM].astype(F32), acc)
                pick_out[kind, cc, :, col:col + DIM] = acc.astype(BF16)
            dev, here = route_to(kind, cc)

            @pl.when(jnp.logical_not(here))
            def _():
                route_copy(kind, cc, c, dev).start()

            @pl.when(here)
            def _():
                pick_in[kind, cc] = pick_out[kind, cc]

    def route_take(kind):
        for cc in range(4):
            @pl.when(jnp.logical_not(jnp.logical_and(c == cc, same) if not kind else c == cc))
            def _():
                route_copy(kind, cc, cc, core).wait_recv()
        return sum(pick_in[kind, cc].astype(F32) for cc in range(4)).astype(BF16)

    def route_drain(kind):
        for cc in range(4):
            dev, here = route_to(kind, cc)

            @pl.when(jnp.logical_not(here))
            def _():
                route_copy(kind, cc, c, dev).wait_send()

    def want_in(zz, cc):
        return jnp.broadcast_to(ints[z * 4 + cc, 0:1, :], (PAGE, DIM)) == zz * 4 + c

    remote(yhi_w(0), yhi_w(0), cross_send.at[NZ], cross_recv.at[NZ], cross).wait_recv()
    z_first(2, yhi_w)
    two_near(0, lat.at[pl.ds(KEEP, PAGE), :])
    z_step(1, own_w, 1, True)
    y_go(-1)
    y_go(1)
    two_second(0)

    @pl.when(apart)
    def _():
        for n in range(2):
            part_taken(n).wait_recv()
            hg.first(n)

    z_step(2, yhi_w, 1, False)
    z_step(1, own_w, 2, True)
    y_go(-2)
    y_go(2)
    cross_take(0)
    swap(1, 0)
    for j in (1, 2, 3):
        src = set_peer(4 - j)
        remote(ints.at[src], ints.at[src], int_send.at[j - 1], int_recv.at[j - 1], core).wait_recv()
    page_load.wait()
    two_last(0)
    route_send(pages, 0, want_in)
    z_step(2, yhi_w, 2, False)
    z_step(1, own_w, 3, True)
    y_go(-3)
    y_go(3)
    hg.second(0, True)
    hg.second(1, False)
    z_step(2, yhi_w, 3, False)
    z_step(1, own_w, 4, True)
    y_go(4)
    hid[pl.ds(pl.multiple_of((k * 4 + x) * TOK + KEEP, 16), PAGE), :] = route_take(0)
    hg.direct(2)
    for dz in (-1, 1, -2, 2):
        y_take(dz)
        swap(0, dz)
        swap(1, dz)
    hg.third(0)
    hg.third(1)
    for dz in (-3, 3):
        y_take(dz)
        swap(0, dz)
        swap(1, dz)
    z_step(2, yhi_w, 4, False)
    y_take(4)
    swap(0, 4)
    swap(1, 4)

    @pl.when(same)
    def _():
        own_loads(lambda copy: copy.wait())

    @pl.when(apart)
    def _():
        shared_copies(lambda copy: copy.wait_recv())

    ends = [info[r, 0:1, 0:1] for r in range(REQS)]

    def segment(pos, bounds):
        seg = jnp.zeros(pos.shape, jnp.int32)
        for r in range(REQS):
            seg = seg + (pos >= bounds[r]).astype(jnp.int32)
        return seg

    kid[:, 0:SEQ] = segment(lax.broadcasted_iota(jnp.int32, (8, SEQ), 1), ends)
    for r in range(REQS):
        j = lax.broadcasted_iota(jnp.int32, (8, TXT), 1)
        kid[:, SEQ + r * TXT:SEQ + (r + 1) * TXT] = jnp.where(j < info[REQS + r, 0:1, 0:1], r, -1)

    wout_load.wait()
    hg.second(2, None)
    hg.third(2)
    for item in (0, 1):
        for dz in range(NZ):
            swap_wait(item, dz)
    for n in range(2):
        hg.last(n)

    def rows_of(start, size=QB):
        return pl.ds(pl.multiple_of(start, 128), size)

    def project(blocks):
        at = [pl.ds(pl.multiple_of(first, 16), size) for first, size in blocks]
        w = jnp.concatenate([wgt[6 * k + n] for n in range(3)] + [wgt[3 + n] for n in range(3)], axis=1)
        a = jnp.concatenate([hid[rows, :] for rows in at], axis=0)
        y = jnp.dot(a, w, preferred_element_type=F32).astype(BF16)
        done = 0
        for rows, (_, size) in zip(at, blocks):
            for n, ref in enumerate((qry, keys, vals)):
                for m in range(2):
                    ref[m, rows, :] = y[done:done + size, (3 * m + n) * DIM:(3 * m + n + 1) * DIM]
            done += size

    def attend(q, pos, m):
        s = lax.dot_general(q, keys[m], (((1,), (1,)), ((), ())), preferred_element_type=F32)
        s = jnp.where(segment(pos, ends) == kid[0:1, :], s, NEG_FILL)
        best = jnp.max(s, axis=1, keepdims=True)
        w = jnp.exp2((s - best) * EXP_SCALE)
        total_w = jnp.sum(w, axis=1, keepdims=True)
        o = jnp.dot(w.astype(BF16), vals[m], preferred_element_type=F32)
        return (o / total_w).astype(BF16)

    def gated(ref, rows, start, heads, bounds, gates):
        size = heads[0].shape[0]
        seg = segment(start + lax.broadcasted_iota(jnp.int32, (size, 1), 0), bounds)
        a = jnp.concatenate(heads, axis=1)

        for n in range(3):
            cols = pl.ds(n * 512, 512)
            proj = jnp.dot(a, wout[:, cols], preferred_element_type=F32)
            scale = gates[3:4, cols]
            for r in (2, 1, 0):
                scale = jnp.where(seg == r, gates[r:r + 1, cols], scale)
            ref[rows, cols] = (ref[rows, cols].astype(F32) + scale * proj).astype(BF16)

    def item_of(n, kk, xx):
        is_b = jnp.logical_or(n == 1, n == 3)
        tok_a = jnp.where(n == 0, 0, jnp.where(n == 2, 2, jnp.where(n == 4, 1, 3)))
        tok_b = kk * 2 + jnp.where(n == 1, 0, 1)
        head = 3 * xx + jnp.where(is_b, 1, 2 * kk)
        return is_b.astype(jnp.int32), head, jnp.where(is_b, tok_b, tok_a) * QB

    def mix_at(n, kk, xx):
        _, head, tok = item_of(n, kk, xx)
        return mix.at[head, rows_of(tok), :]

    mg = Gather(mg_send, mg_recv, mix_at)

    def project_kept(t, carry):
        project([(2 * t * TOK, KEEP), ((2 * t + 1) * TOK, KEEP)])
        return carry

    lax.fori_loop(0, 4, project_kept, 0)
    hg.last(2)
    project([(d * TOK + KEEP, PAGE) for d in range(8)])

    def step_one(n, carry):
        m, head, tok = item_of(n, k, x)
        pos = tok + lax.broadcasted_iota(jnp.int32, (QB, 1), 0)
        mix[head, rows_of(tok), :] = attend(qry[m, rows_of(tok), :], pos, m)
        mg.first(n)

        @pl.when(n >= 2)
        def _():
            mg.second(n - 2, (n - 2) % 2 == 0)
        return carry

    lax.fori_loop(0, 6, step_one, 0)

    def widen(t):
        rows = rows_of(t * QB)
        gated(hid, rows, t * QB, [mix[h, rows, :] for h in range(HEADS)], ends, gate_w)
        project([(t * QB, QB)])

    for n in range(3):
        hg.drain(n)
    mg.third(0)
    mg.third(1)
    mg.last(0)
    mg.last(1)
    mg.second(4, True)
    widen(0)
    mg.second(5, False)
    mg.third(2)
    mg.third(3)
    mg.last(2)
    widen(2)
    mg.third(4)
    mg.third(5)
    mg.last(3)
    mg.last(4)
    widen(1)
    mg.last(5)
    widen(3)

    home_local = pltpu.make_async_copy(hid.at[rows_of(p * TOK, TOK), :], home, home_recv)
    home_copy = remote(hid.at[rows_of(p4 * TOK, TOK), :], home, home_send, home_recv, partner)

    @pl.when(same)
    def _():
        home_local.start()

    @pl.when(apart)
    def _():
        home_copy.start()

    def send_home(src, dst, send, recv, d, sent):
        here = jnp.logical_and(same, d == p)

        if not sent:
            @pl.when(here)
            def _():
                pltpu.make_async_copy(src, dst, recv).start()

        @pl.when(jnp.logical_not(here))
        def _():
            copy = remote(src, dst, send, recv, (work_g, d))
            if sent:
                copy.wait_send()
            else:
                copy.start()

    def page_piece(n, sent):
        head = 3 * x + jnp.where(n < 8, 2 * k, 1)
        d = jnp.where(n < 8, n, k * 4 + n - 8)
        send_home(mine_page.at[n], fin_page.at[head], pa_send.at[n], pa_recv.at[head], d, sent)

    def piece(n, half, sent):
        m = (n >= 4).astype(jnp.int32)
        head = 3 * x + jnp.where(n < 4, 2 * k, 1)
        d = jnp.where(n < 4, 2 * n, k * 4 + 2 * (n - 4)) + half
        send_home(mine.at[n, half], fin.at[head], aa_send.at[n, half], aa_recv.at[head], d, sent)
        return m, d

    def block_pos(rows, block, first):
        i = lax.broadcasted_iota(jnp.int32, (rows, 1), 0)
        return first + i + (i // block) * (TOK - block)

    for m, count, first in ((0, 8, 0), (1, 4, k * 4)):
        q = jnp.concatenate(
            [qry[m, pl.ds(pl.multiple_of((first + j) * TOK + KEEP, 16), PAGE), :] for j in range(count)], axis=0)
        o = attend(q, block_pos(count * PAGE, PAGE, first * TOK + KEEP), m)
        for j in range(count):
            mine_page[8 * m + j] = o[j * PAGE:(j + 1) * PAGE]

    def send_page(n, carry):
        page_piece(n, False)
        return carry

    lax.fori_loop(0, 12, send_page, 0)

    def step_two(n, carry):
        m = (n >= 4).astype(jnp.int32)
        d = jnp.where(n < 4, 2 * n, k * 4 + 2 * (n - 4))
        q = jnp.concatenate(
            [qry[m, pl.ds(pl.multiple_of((d + j) * TOK, 128), KEEP), :] for j in range(2)], axis=0)
        o = attend(q, block_pos(2 * KEEP, KEEP, d * TOK), m)
        for half in (0, 1):
            mine[n, half] = o[half * KEEP:(half + 1) * KEEP]
        for half in (0, 1):
            piece(n, half, False)
        return carry

    def take_heads(ref, recv):
        def take(h, carry):
            remote(ref.at[h], ref.at[h], aa_send.at[0, 0], recv.at[h], core).wait_recv()
            return carry

        lax.fori_loop(0, HEADS, take, 0)

    lax.fori_loop(0, 2, step_two, 0)
    take_heads(fin_page, pa_recv)
    home_copy.wait_recv()
    gated(home, pl.ds(KEEP, PAGE), p * TOK + KEEP, [fin_page[h] for h in range(HEADS)], own_ends, gate)
    back[z, :, 0:WIDTH] = home[KEEP:TOK, :]
    back[z, :, WIDTH:] = jnp.full((PAGE, TAG), inc[0, 0], jnp.int32).astype(F32).astype(BF16)

    two_first(3)
    lax.fori_loop(2, 4, step_two, 0)
    two_near(3)
    lax.fori_loop(4, 6, step_two, 0)
    two_second(3)
    take_heads(fin, aa_recv)
    gated(home, pl.ds(0, KEEP), p * TOK, [fin[h] for h in range(HEADS)], own_ends, gate)
    out[0:KEEP, :] = home[0:KEEP, :]
    two_last(3)

    def want_back(zz, cc):
        return back[zz, :, WIDTH:].astype(F32) == (z * 4 + cc).astype(F32)

    route_send(back, 1, want_back)
    out[KEEP:TOK, :] = route_take(1)

    for copy in pending:
        copy.wait_send()
    route_drain(0)
    route_drain(1)

    @pl.when(same)
    def _():
        shared_copies(lambda copy: copy.wait_send())

    @pl.when(apart)
    def _():
        home_copy.wait_send()
        for n in range(2):
            part_copy(n).wait_send()

    def drain(n, carry):
        mg.drain(n)
        for half in (0, 1):
            piece(n, half, True)
            page_piece(2 * n + half, True)
        return carry

    lax.fori_loop(0, 6, drain, 0)


def pinned(array):
    return pltpu.with_memory_space_constraint(array, pltpu.HBM)


def shards(latent, incoming, req_pages, text_len, gate_scale, text_keys, text_values, w_query, w_key, w_value, w_out):
    vm = pl.BlockSpec(memory_space=pltpu.VMEM)
    hb = pl.BlockSpec(memory_space=pltpu.HBM)
    dma = pltpu.SemaphoreType.DMA
    return pl.pallas_call(
        kernel,
        out_shape=jax.ShapeDtypeStruct((TOK, WIDTH), BF16),
        in_specs=[hb] * 11,
        out_specs=vm,
        scratch_shapes=[
            pltpu.VMEM((SEQ, WIDTH), BF16),
            pltpu.VMEM((TOK, WIDTH), BF16),
            pltpu.VMEM((BLOCKS, WIDTH, DIM), BF16),
            pltpu.VMEM((WIDTH, WIDTH), BF16),
            pltpu.VMEM((HEADS, SEQ, DIM), BF16),
            pltpu.VMEM((2, KEYS, DIM), BF16),
            pltpu.VMEM((2, KEYS, DIM), BF16),
            pltpu.VMEM((2, SEQ, DIM), BF16),
            pltpu.VMEM((6, 2, KEEP, DIM), BF16),
            pltpu.VMEM((HEADS, KEEP, DIM), BF16),
            pltpu.VMEM((12, PAGE, DIM), BF16),
            pltpu.VMEM((HEADS, PAGE, DIM), BF16),
            pltpu.VMEM((8, KEYS), jnp.int32),
            pltpu.VMEM((NZ, PAGE, WIDTH), BF16),
            pltpu.VMEM((NZ, PAGE, WIDTH + TAG), BF16),
            pltpu.VMEM((32, 8, 128), jnp.int32),
            pltpu.VMEM((2, 4, PAGE, WIDTH), BF16),
            pltpu.VMEM((2, 4, PAGE, WIDTH), BF16),
            pltpu.VMEM((2 * REQS, 8, 128), jnp.int32),
            pltpu.VMEM((REQS, WIDTH), F32),
            pltpu.SMEM((1, 1), jnp.int32),
            pltpu.SMEM((1, REQS), jnp.int32),
            pltpu.SMEM((1, REQS), jnp.int32),
            pltpu.VMEM((REQS, WIDTH), F32),
            dma((12,)), dma((BLOCKS,)),
            dma((4, 8)), dma((4, 8)),
            dma((2, NZ)), dma((2, NZ)),
            dma((NZ + 1,)), dma((NZ + 1,)),
            dma((NZ,)), dma((NZ,)),
            dma((3,)), dma((3,)),
            dma((2, 4)), dma((2, 4)),
            dma((2,)), dma((2,)),
            dma((6,)), dma((6,)),
            dma((3, 7)), dma((3, 7)),
            dma((6, 7)), dma((6, 7)),
            dma, dma,
            dma((6, 2)), dma((HEADS,)),
            dma((12,)), dma((HEADS,)),
        ],
        compiler_params=pltpu.CompilerParams(
            collective_id=0, has_side_effects=True, vmem_limit_bytes=50 * 1024 * 1024),
        cost_estimate=pl.CostEstimate(flops=14_000_000_000, bytes_accessed=10_000_000, transcendentals=5_000_000),
    )(
        pinned(latent),
        incoming,
        pinned(req_pages),
        pinned(text_len),
        pinned(gate_scale[0]),
        pinned(text_keys.reshape(REQS * TXT, WIDTH)),
        pinned(text_values.reshape(REQS * TXT, WIDTH)),
        pinned(w_query),
        pinned(w_key),
        pinned(w_value),
        pinned(w_out),
    )


def solution(mesh):
    in_specs = (
        P(("grp", "patch"), None),
        P("patch", "grp"),
        P("grp", None),
        P("grp", None),
        P("grp", None, None),
        P("grp", None, None, None),
        P("grp", None, None, None),
        P("grp", None),
        P("grp", None),
        P("grp", None),
        P(),
    )
    return jax.shard_map(
        shards, mesh=mesh, in_specs=in_specs, out_specs=P(("grp", "patch"), None), check_vma=False)
```
